512 devices in a mesh: chan: 32 (over z_lo, x, core), seg: 16 (over y, z_hi).
Axes of the slice: x: 4, y: 8, z: 8 (z_hi: 2, z_lo: 4; z = z_hi * 4 + z_lo), core: 2. Of those that a mesh axis runs over, the one named last changes fastest.
Arguments:
- strain: float32 [2048, 16, 2048], P('chan', 'seg'), may hold values from -200 to 200
- validity: int32 [2048, 16], P('chan', 'seg'), may hold values from 0 to 1, as said below
- plan: int32 [2], replicated, may hold values from 1 to 3, as said below
Outputs:
- correlations: float32 [2, 2048, 64, 401], P(None, ('chan', 'seg'))
The draws below stay inside these ranges and needn't reach their ends.
Inputs may be any that keep to these rules, and one draw needn't show every extreme that they name: `plan`: distinct pairing offsets. `validity`: some channels are unusable in every segment.
All inputs are finite; a program needn't handle non-finite values.
Results may differ from the reference program's by a relative error of at most 0.0044.
Values may be sent and summed in bfloat16 or wider, within the bound.
A program may use at most 64 MiB of HBM per device.

```python
import math
import jax
import jax.numpy as jnp
from jax import lax

SAMPLES = 2048
BINS = 1024
SMOOTH = 32
HALF_LAGS = 200
LAGS = 401
CB = 64
ROUNDS = 2
REACH_BITS = 2
CHANNELS = 2048
SEGMENTS = 16
N_CHAN = 32


def draw_strain(key, part):
    key = jax.random.fold_in(key, 1)
    subkeys = jax.random.split(key, 3)
    gain_chan = jnp.exp(jax.random.uniform(subkeys[0], (CHANNELS, 1, 1), jnp.float32, 0.0, math.log(10.0)))
    gain_seg = jnp.exp(jax.random.uniform(subkeys[1], (1, SEGMENTS, 1), jnp.float32, 0.0, math.log(3.0)))
    signal = jax.random.truncated_normal(subkeys[2], -6.0, 6.0, (CHANNELS, SEGMENTS, SAMPLES), jnp.float32)
    return signal * gain_chan * gain_seg


def draw_validity(key, part):
    key = jax.random.fold_in(key, 2)
    subkeys = jax.random.split(key, 3)
    dice_rolls = jax.random.randint(subkeys[0], (CHANNELS, SEGMENTS), 0, 1000)
    position = jnp.arange(SEGMENTS, dtype=jnp.int32)
    threshold = 300 + 600 * position // max(SEGMENTS - 1, 1)
    working = jax.random.randint(subkeys[1], (CHANNELS, 1), 0, 16) > 0
    forced = jax.random.randint(subkeys[2], (), 0, CHANNELS)
    working = working & (jnp.arange(CHANNELS, dtype=jnp.int32)[:, None] != forced)
    return ((dice_rolls < threshold[None, :]) & working).astype(jnp.int32)


def draw_plan(key, part):
    key = jax.random.fold_in(key, 3)
    subkeys = jax.random.split(key, 2)
    largest = 2 ** REACH_BITS - 1
    others = jax.random.permutation(subkeys[0], largest - 1)[:ROUNDS - 1] + 1
    offsets = jnp.concatenate([others.astype(jnp.int32), jnp.full((1,), largest, jnp.int32)])
    return jax.random.permutation(subkeys[1], offsets).astype(jnp.int32)


def setup_inputs(seed: int = 0) -> dict:
    seeds = jax.random.split(jax.random.key(seed), 4)
    strain = draw_strain(jax.random.fold_in(seeds[3], 71), 0)
    validity = draw_validity(jax.random.fold_in(seeds[3], 71), 0)
    plan = draw_plan(jax.random.fold_in(seeds[3], 71), 0)
    return {"strain": strain, "validity": validity, "plan": plan}


EPSILON = 1e-05

def lag_table(first_bin, bin_count, samples, total_bins):
    bin_index = first_bin + 1 + jnp.arange(bin_count, dtype=jnp.int32)
    lag_index = jnp.arange(-HALF_LAGS, HALF_LAGS + 1, dtype=jnp.int32)
    angles = jnp.mod(bin_index[:, None] * lag_index[None, :], samples).astype(jnp.float32) * (2.0 * math.pi / samples)
    weight = 2.0 / math.sqrt(total_bins)
    return jnp.concatenate([weight * jnp.cos(angles), -weight * jnp.sin(angles)], axis=0)

def whiten(spectrum, weights):
    magnitude = jnp.sqrt(spectrum[:, 0] * spectrum[:, 0] + spectrum[:, 1] * spectrum[:, 1])
    window = 2 * SMOOTH + 1
    summed = lax.reduce_window(magnitude, jnp.zeros((), magnitude.dtype), lax.add, (1, window), (1, 1), ((0, 0), (SMOOTH, SMOOTH)))
    smoothed = summed / window
    factor = weights[:, None] / (smoothed + EPSILON)
    return (spectrum * factor[:, None, :]).astype(jnp.bfloat16)

def block_lags(own_block, partner_block, lag_weights):
    highest = lax.Precision.HIGHEST
    own_block = own_block.astype(jnp.float32)
    partner_block = partner_block.astype(jnp.float32)
    real_real = jnp.einsum('isk,jsk->ijk', own_block[:, :, 0], partner_block[:, :, 0], precision=highest)
    imag_imag = jnp.einsum('isk,jsk->ijk', own_block[:, :, 1], partner_block[:, :, 1], precision=highest)
    imag_real = jnp.einsum('isk,jsk->ijk', own_block[:, :, 1], partner_block[:, :, 0], precision=highest)
    real_imag = jnp.einsum('isk,jsk->ijk', own_block[:, :, 0], partner_block[:, :, 1], precision=highest)
    spectral = jnp.concatenate([real_real + imag_imag, imag_real - real_imag], axis=2)
    own_count = spectral.shape[0]
    partner_count = spectral.shape[1]
    lagged = jnp.dot(spectral.reshape(own_count * partner_count, -1), lag_weights, precision=highest, preferred_element_type=jnp.float32)
    return lagged.reshape(own_count, partner_count, -1)

def reference(strain, validity, plan):
    spectrum = jnp.fft.rfft(strain, axis=-1)[..., 1:]
    stacked_parts = jnp.stack([jnp.real(spectrum), jnp.imag(spectrum)], axis=2)
    flattened = stacked_parts.reshape(CHANNELS * SEGMENTS, 2, BINS)
    weights = validity.astype(jnp.float32).reshape(-1)
    whitened = whiten(flattened, weights).reshape(CHANNELS, SEGMENTS, 2, BINS)
    mask_all = validity.astype(jnp.float32)
    lag_weights = lag_table(0, BINS, SAMPLES, BINS)

    def one_round(offset):

        def one_block(block_number):
            own_start = (block_number * CB).astype(jnp.int32)
            partner_start = (jnp.mod(block_number - offset, N_CHAN) * CB).astype(jnp.int32)
            own_block = lax.dynamic_slice_in_dim(whitened, own_start, CB, 0)
            partner_block = lax.dynamic_slice_in_dim(whitened, partner_start, CB, 0)
            own_mask = lax.dynamic_slice_in_dim(mask_all, own_start, CB, 0)
            partner_mask = lax.dynamic_slice_in_dim(mask_all, partner_start, CB, 0)
            counts = jnp.dot(own_mask, partner_mask.T, precision=lax.Precision.HIGHEST, preferred_element_type=jnp.float32)
            stacked = block_lags(own_block, partner_block, lag_weights)
            return stacked / jnp.maximum(counts, 1.0)[:, :, None]
        return lax.map(one_block, jnp.arange(N_CHAN, dtype=jnp.int32))
    rounds_out = lax.map(one_round, plan)
    return rounds_out.reshape(ROUNDS, CHANNELS, CB, LAGS)
```

```python
import math

import jax
import jax.numpy as jnp
import ml_dtypes
import numpy as np
from jax import lax
from jax.experimental import pallas as pl
from jax.experimental.pallas import tpu as pltpu
from jax.sharding import PartitionSpec as P

MESH = pl.DeviceIdType.MESH
SMOOTH = 32
HALF_LAGS = 200
LAGS = 2 * HALF_LAGS + 1
SAMPLES = 2048
BINS = 1024
EPSILON = 1e-05
ROUNDS = 2
F32 = jnp.float32
BF16 = jnp.bfloat16


def place(r):
    if r == 8 or r == 16:
        return 0, r // 16
    return (r, 0) if r < 8 else (16 - r, 1)


def split(table):
    high = table.astype(ml_dtypes.bfloat16)
    low = (table - high.astype(np.float64)).astype(ml_dtypes.bfloat16)
    return high, low


def dft_tables():
    c = np.arange(128)[:, None]
    q = np.arange(64)[None, :]

    def angle(steps, period):
        return 2.0 * np.pi * np.mod(steps, period) / period

    low, high = angle(c * q, 128), angle(c * (127 - q), 128)
    first = np.zeros((256, 256))
    first[:128, 0:64], first[128:, 0:64] = np.cos(low), np.sin(low)
    first[:128, 64:128], first[128:, 64:128] = -np.sin(low), np.cos(low)
    first[:128, 128:192], first[128:, 128:192] = np.cos(high), np.sin(high)
    first[:128, 192:256], first[128:, 192:256] = np.sin(high), -np.cos(high)
    eight, sixteen = angle(c * (8 + 16 * q), SAMPLES), angle(c * (16 + 16 * q), SAMPLES)
    second = np.zeros((256, 256))
    second[128:, 0:64], second[128:, 64:128] = np.cos(eight), -np.sin(eight)
    second[:128, 128:192], second[:128, 192:256] = np.cos(sixteen), -np.sin(sixteen)
    turn = angle(np.arange(8)[:, None] * np.arange(128)[None, :], SAMPLES)
    twiddle = np.concatenate([np.cos(turn), np.sin(turn)], axis=0).astype(np.float32)
    return split(first) + split(second) + (twiddle,)


def lag_table():
    lag = np.arange(-HALF_LAGS, HALF_LAGS + 1)[None, :]
    weight = 2.0 / math.sqrt(BINS)
    table = np.zeros((8, 256, 512))
    for r in range(1, 17):
        slab, half = place(r)
        turn = 2.0 * np.pi * np.mod((r + 16 * np.arange(64)[:, None]) * lag, SAMPLES) / SAMPLES
        table[slab, 128 * half : 128 * half + 64, :LAGS] = weight * np.cos(turn)
        table[slab, 128 * half + 64 : 128 * half + 128, :LAGS] = -weight * np.sin(turn)
    return table.astype(ml_dtypes.bfloat16)


def first_stage(x):
    root = math.sqrt(0.5)
    e = [x[a] + x[a + 8] for a in range(8)]
    o = [x[a] - x[a + 8] for a in range(8)]
    ee = [e[a] + e[a + 4] for a in range(4)]
    eo = [e[a] - e[a + 4] for a in range(4)]
    y = {}
    even, odd = ee[0] + ee[2], ee[1] + ee[3]
    y[0], y[8] = even + odd, even - odd
    y[4] = (ee[0] - ee[2], ee[3] - ee[1])
    minus, plus = root * (eo[1] - eo[3]), root * (eo[1] + eo[3])
    y[2] = (eo[0] + minus, -(eo[2] + plus))
    y[6] = (eo[0] - minus, eo[2] - plus)
    dm = [None] + [o[a] - o[8 - a] for a in (1, 2, 3)]
    dp = [None] + [o[a] + o[8 - a] for a in (1, 2, 3)]
    for k in (1, 3, 5, 7):
        real, imag = o[0], o[4] * math.sin(math.pi * k / 2)
        for a in (1, 2, 3):
            real = real + math.cos(2 * math.pi * a * k / 16) * dm[a]
            imag = imag + math.sin(2 * math.pi * a * k / 16) * dp[a]
        y[k] = (real, -imag)
    return y


def kernel(
    plan, x, valid, t1h, t1l, t2h, t2l, twiddle, lag_hbm, out,
    zh_, zl_, spec, ws, zw, wg, v, fl, fv, fpad, fto, ctab, crecv, inv,
    a_, b_, c_, d_, xs, xr, lag, keep, zs, zr,
    lag_sem, y1s, y1r, zws, zwr, y2s, y2r, p_s, p_r, f1s, f1r, fxs, fxr, cs, cr, ys, yr, zss, zrr,
):
    chan, seg = lax.axis_index("chan"), lax.axis_index("seg")
    core = lax.rem(chan, 2)
    y, zh = seg // 2, lax.rem(seg, 2)
    oz = 1 - zh
    kappa = lax.rem(y, 4)

    def at_y(step):
        return lax.rem(y + step, 8)

    def chan_at(step):
        return lax.rem(chan + step + 32, 32)

    def on_y(row):
        return (chan, 2 * row + zh)

    other = (chan, 2 * y + oz)
    ahead = (chan_at(2), seg)
    jump = (chan_at(1 + 2 * core), seg)
    mate = (chan_at(1 - 2 * core), seg)

    def remote(src, dst, send, recv, device):
        return pltpu.make_async_remote_copy(
            src_ref=src, dst_ref=dst, send_sem=send, recv_sem=recv, device_id=device, device_id_type=MESH
        )

    barrier = pltpu.get_barrier_semaphore()
    senders = [on_y(at_y(s)) for s in range(1, 8)] + [other]
    senders += [(chan_at(-2), seg), (chan_at(-3 + 2 * core), seg), mate]
    for device in senders:
        pl.semaphore_signal(barrier, inc=1, device_id=device, device_id_type=MESH)
    lag_copy = pltpu.make_async_copy(lag_hbm.at[pl.ds(4 * zh, 4)], lag, lag_sem)
    lag_copy.start()

    def transform(g, carry):
        rows = pl.ds(pl.multiple_of(g * 16, 16), 16)
        ys_ = first_stage([x[rows, 128 * s : 128 * s + 128] for s in range(16)])
        pairs = [(ys_[0], ys_[8])]
        for k in range(1, 8):
            real, imag = ys_[k]
            co, si = twiddle[k : k + 1, :], twiddle[8 + k : 9 + k, :]
            pairs.append((real * co + imag * si, imag * co - real * si))
        for j in range(8):
            for part in range(2):
                high = pairs[j][part].astype(BF16)
                zh_[j, rows, 128 * part : 128 * part + 128] = high
                zl_[j, rows, 128 * part : 128 * part + 128] = (pairs[j][part] - high.astype(F32)).astype(BF16)
        return carry

    lax.fori_loop(0, 4, transform, 0)

    def product(high, low, th, tl):
        total = jnp.dot(high, tl[...], preferred_element_type=F32)
        total += jnp.dot(low, th[...], preferred_element_type=F32)
        return total + jnp.dot(high, th[...], preferred_element_type=F32)

    spec[0] = product(zh_[0], zl_[0], t2h, t2l)
    main = product(zh_[1:8].reshape(448, 256), zl_[1:8].reshape(448, 256), t1h, t1l)
    spec[1:8] = main.reshape(7, 64, 256)

    lane = lax.broadcasted_iota(jnp.int32, (16, 128), 1)
    q = jnp.bitwise_and(lane, 63)

    def shifted(value, by):
        moved = pltpu.roll(value, (128 - by) % 128, 1)
        kept = q < 64 - by if by > 0 else q >= -by
        return jnp.where(kept, moved, 0.0)

    def whiten(g, carry):
        rows = pl.ds(pl.multiple_of(g * 16, 16), 16)
        mags = []
        for r in range(1, 17):
            slab, half = place(r)
            value = spec[slab, rows, 128 * half : 128 * half + 128]
            square = value * value
            mags.append(jnp.sqrt(square + pltpu.roll(square, 64, 1)))
        below, above = [mags[0]], [mags[15]]
        for r in range(1, 16):
            below.append(below[-1] + mags[r])
            above.append(above[-1] + mags[15 - r])
        above = above[::-1]
        whole = below[15]
        middle = shifted(whole, -1) + whole + shifted(whole, 1)
        weight = valid[rows, :].astype(F32)
        for r in range(1, 17):
            slab, half = place(r)
            window = shifted(above[r - 1], -2) + middle + shifted(below[r - 1], 2)
            factor = weight / (window * (1.0 / (2 * SMOOTH + 1)) + EPSILON)
            value = spec[slab, rows, 128 * half : 128 * half + 128]
            ws[slab, g, :, 128 * half : 128 * half + 128] = (value * factor).astype(BF16)
        return carry

    lax.fori_loop(0, 4, whiten, 0)
    column = jnp.broadcast_to(valid[...].astype(F32), (64, 128))
    fl[y] = jnp.transpose(jnp.concatenate([column, column], axis=0))[0:1, :]

    pl.semaphore_wait(barrier, 11)

    z_sends, y1_sends, y2_sends, f_sends = [], [], [], []
    for step in range(4):
        k = lax.rem(kappa + step, 4)
        z_sends.append(remote(ws.at[4 * oz + k], zw.at[k], zws.at[k], zwr.at[k], other))
        z_sends[-1].start()
    for step in (4, 3, 5, 2, 6, 1, 7):
        row = at_y(step)
        y1_sends.append(
            remote(ws.at[4 * zh + lax.rem(row, 4)], wg.at[zh, :, y], y1s.at[step], y1r.at[step], on_y(row))
        )
        y1_sends[-1].start()
    for step in range(1, 8):
        f_sends.append(remote(fl.at[y], fl.at[y], f1s.at[step], f1r.at[step], on_y(at_y(step))))
        f_sends[-1].start()
    wg[zh, :, y] = ws[4 * zh + kappa]

    def put_p1(half, j):
        piece = wg.at[half, j]
        first = remote(piece, v.at[1, half, j], p_s.at[0, half, j], p_r.at[1, half, j], ahead)
        second = remote(
            piece, v.at[2 * core, half, j], p_s.at[1, half, j], p_r.at[2 * core, half, j], jump
        )
        return first, second

    def put_p2(half, j):
        return remote(
            v.at[1, half, j], v.at[2 - 2 * core, half, j], p_s.at[2, half, j], p_r.at[2 - 2 * core, half, j], mate
        )

    def arrived(slot, half, j):
        remote(v.at[slot, half, j], v.at[slot, half, j], p_s.at[0, half, j], p_r.at[slot, half, j], ahead).wait_recv()

    for copy in y1_sends:
        copy.wait_recv()

    def start_p1(half):
        def body(j, carry):
            for copy in put_p1(half, j):
                copy.start()
            return carry

        lax.fori_loop(0, 4, body, 0)

    start_p1(zh)
    for step in range(4):
        k = lax.rem(kappa + step, 4)
        z_sends[step].wait_recv()
        for far in (4, 0):
            if step + far == 0:
                wg[oz, :, y] = zw[k]
                continue
            row = at_y(step + far)
            y2_sends.append(
                remote(zw.at[k], wg.at[oz, :, y], y2s.at[step + far], y2r.at[step + far], on_y(row))
            )
            y2_sends[-1].start()

    for copy in f_sends:
        copy.wait_recv()
    flag_sends = [
        remote(fl, fv.at[1], fxs.at[0], fxr.at[1], ahead),
        remote(fl, fv.at[2 * core], fxs.at[1], fxr.at[2 * core], jump),
    ]
    for copy in flag_sends:
        copy.start()

    def start_p2(j, carry):
        arrived(1, zh, j)
        put_p2(zh, j).start()
        return carry

    lax.fori_loop(0, 4, start_p2, 0)
    for copy in y2_sends:
        copy.wait_recv()
    start_p1(oz)

    remote(fv.at[1], fv.at[1], fxs.at[0], fxr.at[1], ahead).wait_recv()
    flag_sends.append(remote(fv.at[1], fv.at[2 - 2 * core], fxs.at[2], fxr.at[2 - 2 * core], mate))
    flag_sends[-1].start()

    first_half = lane < 64
    sign = jnp.where(first_half, 1.0, -1.0).astype(F32)

    def spread(s, carry):
        half, row = s // 8, lax.rem(s, 8)
        for j in range(4):
            value = wg[half, j, row].astype(F32)
            for h in range(2):
                one = value[:, 128 * h : 128 * h + 128]
                swapped = pltpu.roll(one, 64, 1)
                a_[s, h, 16 * j : 16 * j + 16, :] = jnp.where(first_half, one, swapped)
                b_[s, h, 16 * j : 16 * j + 16, :] = jnp.where(first_half, swapped, one)
        return carry

    lax.fori_loop(0, 16, spread, 0)

    def chosen(r, options):
        offset = plan[r]
        return jnp.where(offset == 1, options[0], jnp.where(offset == 2, options[1], options[2]))

    def prepare(r, j):
        def body(s, carry):
            half, row = s // 8, lax.rem(s, 8)
            value = chosen(r, [v[d, half, j, row].astype(F32) for d in range(3)])
            for h in range(2):
                one = value[:, 128 * h : 128 * h + 128]
                c_[s, h] = one * sign
                d_[s, h] = pltpu.roll(one, 64, 1)
            return carry

        lax.fori_loop(0, 16, body, 0)

    hops = [2 + 4 * core, 1, 7, 0]

    def cross(r, j, t, target):
        start = pl.multiple_of(8 * at_y(hops[t]), 8)
        for h in range(2):

            def body(s, totals):
                c, d = c_[s, h], d_[s, h]
                mine = [
                    a_[s, h, pl.ds(start + i, 1), :] * c + b_[s, h, pl.ds(start + i, 1), :] * d
                    for i in range(8)
                ]
                return tuple(total + one for total, one in zip(totals, mine))

            totals = lax.fori_loop(0, 16, body, (jnp.zeros((16, 128), F32),) * 8, unroll=2)
            for i in range(8):
                target[16 * i : 16 * i + 16, 128 * h : 128 * h + 128] = totals[i].astype(BF16)

    def put_cross(r, j, t):
        return remote(
            xs.at[r, j, t], xr.at[r, j, kappa], ys.at[r, j, t], yr.at[r, j, t], on_y(at_y(hops[t]))
        )

    def cross_all(r, j):
        prepare(r, j)
        for t in range(3):
            cross(r, j, t, xs.at[r, j, t])
            put_cross(r, j, t).start()
        cross(r, j, 3, xr.at[r, j, kappa])

    def put_lags(r, j):
        return remote(zs.at[r, j], zr.at[r, j], zss.at[r, j], zrr.at[r, j], other)

    def lagged(r, j, side):
        rows = pl.ds(pl.multiple_of(64 * side, 64), 64)
        total = jnp.dot(xr[r, j, 0, rows, :], lag[0], preferred_element_type=F32)
        for k in range(1, 4):
            total += jnp.dot(xr[r, j, k, rows, :], lag[k], preferred_element_type=F32)
        return total

    def lag_stage(r, j):
        for t in range(3):
            put_cross(r, j, t).wait_recv()
        zs[r, j] = lagged(r, j, oz).astype(BF16)
        put_lags(r, j).start()
        keep[r, j] = lagged(r, j, zh)

    def finish(r, j):
        put_lags(r, j).wait_recv()
        total = keep[r, j] + zr[r, j].astype(F32)
        rows = pl.ds(pl.multiple_of(16 * j, 16), 16)
        for i in range(4):
            scale = inv[r, i, rows, 0:1]
            out[r, i, rows, :] = (total[16 * i : 16 * i + 16, :] * scale)[:, :LAGS]

    def start_round(j):
        arrived(1, oz, j)
        put_p2(oz, j).start()

    start_round(0)

    wide = lax.broadcasted_iota(jnp.int32, (64, 128), 1)
    fpad[...] = jnp.zeros((128, 128), F32)
    for s in range(8):
        fpad[s : s + 1, :] = fl[s]
    fto[...] = jnp.transpose(fpad[...])
    remote(fv.at[0], fv.at[0], fxs.at[0], fxr.at[0], ahead).wait_recv()
    remote(fv.at[2], fv.at[2], fxs.at[0], fxr.at[2], ahead).wait_recv()
    table = jnp.zeros((64, 128), F32)
    for r in range(ROUNDS):
        for s in range(8):
            fpad[s : s + 1, :] = chosen(r, [fv[d, s] for d in range(3)])
        partner = jnp.transpose(fpad[...])[0:64, :]
        for i in range(8):
            number = jnp.sum(partner * fto[pl.ds(8 * y + i, 1), :], axis=1, keepdims=True)
            table = jnp.where(wide == 8 * r + i, number, table)
    ctab[...] = table
    count_send = remote(ctab, crecv, cs, cr, other)
    count_send.start()

    lag_copy.wait()

    def main_loop(j, carry):
        arrived(0, zh, j)
        arrived(0, oz, j)
        arrived(2, zh, j)
        arrived(2, oz, j)
        cross_all(0, j)

        @pl.when(j < 3)
        def _():
            start_round(j + 1)

        cross_all(1, j)

        @pl.when(j == 1)
        def _():
            count_send.wait_recv()
            both = ctab[...] + crecv[...]
            for r in range(ROUNDS):
                for i in range(4):
                    number = jnp.sum(
                        jnp.where(wide == 8 * r + 4 * zh + i, both, 0.0), axis=1, keepdims=True
                    )
                    inv[r, i] = jnp.broadcast_to(1.0 / jnp.maximum(number, 1.0), (64, 128))

        @pl.when(j >= 1)
        def _():
            for r in range(ROUNDS):
                lag_stage(r, j - 1)

        @pl.when(j >= 2)
        def _():
            for r in range(ROUNDS):
                finish(r, j - 2)

        return carry

    lax.fori_loop(0, 4, main_loop, 0)
    for r in range(ROUNDS):
        lag_stage(r, 3)
    for j in (2, 3):
        for r in range(ROUNDS):
            finish(r, j)

    for copy in z_sends + y1_sends + y2_sends + f_sends + flag_sends + [count_send]:
        copy.wait_send()

    def drain(j, carry):
        for half in range(2):
            for copy in put_p1(half, j):
                copy.wait_send()
            put_p2(half, j).wait_send()
        for r in range(ROUNDS):
            for t in range(3):
                put_cross(r, j, t).wait_send()
            put_lags(r, j).wait_send()
        return carry

    lax.fori_loop(0, 4, drain, 0)


def shards(strain, validity, plan):
    t1h, t1l, t2h, t2l, twiddle = (jnp.asarray(t) for t in dft_tables())
    lag = jnp.asarray(lag_table())
    vmem = pl.BlockSpec(memory_space=pltpu.VMEM)
    dma = pltpu.SemaphoreType.DMA
    return pl.pallas_call(
        kernel,
        out_shape=jax.ShapeDtypeStruct((ROUNDS, 4, 64, LAGS), F32),
        in_specs=[pl.BlockSpec(memory_space=pltpu.SMEM)] + [vmem] * 7 + [pl.BlockSpec(memory_space=pl.ANY)],
        out_specs=vmem,
        scratch_shapes=[
            pltpu.VMEM((8, 64, 256), BF16),
            pltpu.VMEM((8, 64, 256), BF16),
            pltpu.VMEM((8, 64, 256), F32),
            pltpu.VMEM((8, 4, 16, 256), BF16),
            pltpu.VMEM((4, 4, 16, 256), BF16),
            pltpu.VMEM((2, 4, 8, 16, 256), BF16),
            pltpu.VMEM((3, 2, 4, 8, 16, 256), BF16),
            pltpu.VMEM((8, 1, 128), F32),
            pltpu.VMEM((3, 8, 1, 128), F32),
            pltpu.VMEM((128, 128), F32),
            pltpu.VMEM((128, 128), F32),
            pltpu.VMEM((64, 128), F32),
            pltpu.VMEM((64, 128), F32),
            pltpu.VMEM((2, 4, 64, 128), F32),
            pltpu.VMEM((16, 2, 64, 128), F32),
            pltpu.VMEM((16, 2, 64, 128), F32),
            pltpu.VMEM((16, 2, 16, 128), F32),
            pltpu.VMEM((16, 2, 16, 128), F32),
            pltpu.VMEM((2, 4, 3, 128, 256), BF16),
            pltpu.VMEM((2, 4, 4, 128, 256), BF16),
            pltpu.VMEM((4, 256, 512), BF16),
            pltpu.VMEM((2, 4, 64, 512), F32),
            pltpu.VMEM((2, 4, 64, 512), BF16),
            pltpu.VMEM((2, 4, 64, 512), BF16),
            dma,
            dma((8,)), dma((8,)),
            dma((4,)), dma((4,)),
            dma((8,)), dma((8,)),
            dma((3, 2, 4)), dma((3, 2, 4)),
            dma((8,)), dma((8,)),
            dma((3,)), dma((3,)),
            dma, dma,
            dma((2, 4, 3)), dma((2, 4, 3)),
            dma((2, 4)), dma((2, 4)),
        ],
        compiler_params=pltpu.CompilerParams(
            collective_id=0, has_side_effects=True, vmem_limit_bytes=40 * 1024 * 1024
        ),
        name="correlate",
    )(plan, strain.reshape(64, SAMPLES), validity, t1h, t1l, t2h, t2l, twiddle, lag)


def solution(mesh):
    placed = (P("chan", "seg", None), P("chan", "seg"), P())
    return jax.shard_map(
        shards,
        mesh=mesh,
        in_specs=placed,
        out_specs=P(None, ("chan", "seg"), None, None),
        check_vma=False,
    )
```

```python
import math

import jax
import jax.numpy as jnp
import ml_dtypes
import numpy as np
from jax import lax
from jax.experimental import pallas as pl
from jax.experimental.pallas import tpu as pltpu
from jax.sharding import PartitionSpec as P

MESH = pl.DeviceIdType.MESH
SMOOTH = 32
HALF_LAGS = 200
LAGS = 2 * HALF_LAGS + 1
SAMPLES = 2048
BINS = 1024
EPSILON = 1e-05
ROUNDS = 2
F32 = jnp.float32
BF16 = jnp.bfloat16


def place(r):
    if r == 8 or r == 16:
        return 0, r // 16
    return (r, 0) if r < 8 else (16 - r, 1)


def split(table):
    high = table.astype(ml_dtypes.bfloat16)
    low = (table - high.astype(np.float64)).astype(ml_dtypes.bfloat16)
    return high, low


def dft_tables():
    c = np.arange(128)[:, None]
    q = np.arange(64)[None, :]

    def angle(steps, period):
        return 2.0 * np.pi * np.mod(steps, period) / period

    low, high = angle(c * q, 128), angle(c * (127 - q), 128)
    first = np.zeros((256, 256))
    first[:128, 0:64], first[128:, 0:64] = np.cos(low), np.sin(low)
    first[:128, 64:128], first[128:, 64:128] = -np.sin(low), np.cos(low)
    first[:128, 128:192], first[128:, 128:192] = np.cos(high), np.sin(high)
    first[:128, 192:256], first[128:, 192:256] = np.sin(high), -np.cos(high)
    eight, sixteen = angle(c * (8 + 16 * q), SAMPLES), angle(c * (16 + 16 * q), SAMPLES)
    second = np.zeros((256, 256))
    second[128:, 0:64], second[128:, 64:128] = np.cos(eight), -np.sin(eight)
    second[:128, 128:192], second[:128, 192:256] = np.cos(sixteen), -np.sin(sixteen)
    turn = angle(np.arange(8)[:, None] * np.arange(128)[None, :], SAMPLES)
    twiddle = np.concatenate([np.cos(turn), np.sin(turn)], axis=0).astype(np.float32)
    return split(first) + split(second) + (twiddle,)


def lag_table():
    lag = np.arange(-HALF_LAGS, HALF_LAGS + 1)[None, :]
    weight = 2.0 / math.sqrt(BINS)
    table = np.zeros((8, 256, 512))
    for r in range(1, 17):
        slab, half = place(r)
        turn = 2.0 * np.pi * np.mod((r + 16 * np.arange(64)[:, None]) * lag, SAMPLES) / SAMPLES
        table[slab, 128 * half : 128 * half + 64, :LAGS] = weight * np.cos(turn)
        table[slab, 128 * half + 64 : 128 * half + 128, :LAGS] = -weight * np.sin(turn)
    return table.astype(ml_dtypes.bfloat16)


def first_stage(x):
    root = math.sqrt(0.5)
    e = [x[a] + x[a + 8] for a in range(8)]
    o = [x[a] - x[a + 8] for a in range(8)]
    ee = [e[a] + e[a + 4] for a in range(4)]
    eo = [e[a] - e[a + 4] for a in range(4)]
    y = {}
    even, odd = ee[0] + ee[2], ee[1] + ee[3]
    y[0], y[8] = even + odd, even - odd
    y[4] = (ee[0] - ee[2], ee[3] - ee[1])
    minus, plus = root * (eo[1] - eo[3]), root * (eo[1] + eo[3])
    y[2] = (eo[0] + minus, -(eo[2] + plus))
    y[6] = (eo[0] - minus, eo[2] - plus)
    dm = [None] + [o[a] - o[8 - a] for a in (1, 2, 3)]
    dp = [None] + [o[a] + o[8 - a] for a in (1, 2, 3)]
    for k in (1, 3, 5, 7):
        real, imag = o[0], o[4] * math.sin(math.pi * k / 2)
        for a in (1, 2, 3):
            real = real + math.cos(2 * math.pi * a * k / 16) * dm[a]
            imag = imag + math.sin(2 * math.pi * a * k / 16) * dp[a]
        y[k] = (real, -imag)
    return y


def kernel(
    plan_in, x_in, valid_in, t1h_in, t1l_in, t2h_in, t2l_in, twiddle_in, lag_in, out,
    plan, x, flags, t1h, t1l, t2h, t2l, twiddle, valid, zh_, zl_, spec, ws, zw, wg, v, fl, fv, fpad, fto, ctab, crecv, inv,
    a_, b_, c_, d_, xs, xr, lag, keep, zs, zr,
    in_sems, y1s, y1r, zws, zwr, y2s, y2r, p_s, p_r, f1s, f1r, fxs, fxr, cs, cr, ys, yr, zss, zrr,
):
    chan, seg = lax.axis_index("chan"), lax.axis_index("seg")
    core = lax.rem(chan, 2)
    y, zh = seg // 2, lax.rem(seg, 2)
    oz = 1 - zh
    kappa = lax.rem(y, 4)

    def at_y(step):
        return lax.rem(y + step, 8)

    def chan_at(step):
        return lax.rem(chan + step + 32, 32)

    def on_y(row):
        return (chan, 2 * row + zh)

    other = (chan, 2 * y + oz)
    ahead = (chan_at(2), seg)
    jump = (chan_at(1 + 2 * core), seg)
    mate = (chan_at(1 - 2 * core), seg)

    def remote(src, dst, send, recv, device):
        return pltpu.make_async_remote_copy(
            src_ref=src, dst_ref=dst, send_sem=send, recv_sem=recv, device_id=device, device_id_type=MESH
        )

    barrier = pltpu.get_barrier_semaphore()
    senders = [on_y(at_y(s)) for s in range(1, 8)] + [other]
    senders += [(chan_at(-2), seg), (chan_at(-3 + 2 * core), seg), mate]
    for device in senders:
        pl.semaphore_signal(barrier, inc=1, device_id=device, device_id_type=MESH)
    loads = [pltpu.make_async_copy(x_in.at[:, 0, :], x, in_sems.at[0])]
    pairs_in = [(twiddle_in, twiddle), (valid_in, flags), (t1h_in, t1h), (t1l_in, t1l), (t2h_in, t2h), (t2l_in, t2l)]
    pairs_in += [(plan_in, plan), (lag_in.at[pl.ds(4 * zh, 4)], lag)]
    for number, (src, dst) in enumerate(pairs_in):
        loads.append(pltpu.make_async_copy(src, dst, in_sems.at[number + 1]))
    for copy in loads:
        copy.start()
    for copy in loads[:3]:
        copy.wait()
    square_flags = jnp.broadcast_to(flags[...].astype(F32), (64, 64))
    valid[...] = jnp.transpose(square_flags)[:, 0:1]

    def transform(g, carry):
        rows = pl.ds(pl.multiple_of(g * 16, 16), 16)
        ys_ = first_stage([x[rows, 128 * s : 128 * s + 128] for s in range(16)])
        pairs = [(ys_[0], ys_[8])]
        for k in range(1, 8):
            real, imag = ys_[k]
            co, si = twiddle[k : k + 1, :], twiddle[8 + k : 9 + k, :]
            pairs.append((real * co + imag * si, imag * co - real * si))
        for j in range(8):
            for part in range(2):
                high = pairs[j][part].astype(BF16)
                zh_[j, rows, 128 * part : 128 * part + 128] = high
                zl_[j, rows, 128 * part : 128 * part + 128] = (pairs[j][part] - high.astype(F32)).astype(BF16)
        return carry

    lax.fori_loop(0, 4, transform, 0)

    for copy in loads[3:8]:
        copy.wait()

    def product(high, low, th, tl):
        total = jnp.dot(high, tl[...], preferred_element_type=F32)
        total += jnp.dot(low, th[...], preferred_element_type=F32)
        return total + jnp.dot(high, th[...], preferred_element_type=F32)

    spec[0] = product(zh_[0], zl_[0], t2h, t2l)
    main = product(zh_[1:8].reshape(448, 256), zl_[1:8].reshape(448, 256), t1h, t1l)
    spec[1:8] = main.reshape(7, 64, 256)

    lane = lax.broadcasted_iota(jnp.int32, (16, 128), 1)
    q = jnp.bitwise_and(lane, 63)

    def shifted(value, by):
        moved = pltpu.roll(value, (128 - by) % 128, 1)
        kept = q < 64 - by if by > 0 else q >= -by
        return jnp.where(kept, moved, 0.0)

    def whiten(g, carry):
        rows = pl.ds(pl.multiple_of(g * 16, 16), 16)
        mags = []
        for r in range(1, 17):
            slab, half = place(r)
            value = spec[slab, rows, 128 * half : 128 * half + 128]
            square = value * value
            mags.append(jnp.sqrt(square + pltpu.roll(square, 64, 1)))
        below, above = [mags[0]], [mags[15]]
        for r in range(1, 16):
            below.append(below[-1] + mags[r])
            above.append(above[-1] + mags[15 - r])
        above = above[::-1]
        whole = below[15]
        middle = shifted(whole, -1) + whole + shifted(whole, 1)
        weight = valid[rows, :]
        for r in range(1, 17):
            slab, half = place(r)
            window = shifted(above[r - 1], -2) + middle + shifted(below[r - 1], 2)
            factor = weight / (window * (1.0 / (2 * SMOOTH + 1)) + EPSILON)
            value = spec[slab, rows, 128 * half : 128 * half + 128]
            ws[slab, g, :, 128 * half : 128 * half + 128] = (value * factor).astype(BF16)
        return carry

    lax.fori_loop(0, 4, whiten, 0)
    column = jnp.broadcast_to(valid[...], (64, 128))
    fl[y] = jnp.transpose(jnp.concatenate([column, column], axis=0))[0:1, :]

    pl.semaphore_wait(barrier, 11)

    z_sends, y1_sends, y2_sends, f_sends = [], [], [], []
    for step in range(4):
        k = lax.rem(kappa + step, 4)
        z_sends.append(remote(ws.at[4 * oz + k], zw.at[k], zws.at[k], zwr.at[k], other))
        z_sends[-1].start()
    for step in (4, 3, 5, 2, 6, 1, 7):
        row = at_y(step)
        y1_sends.append(
            remote(ws.at[4 * zh + lax.rem(row, 4)], wg.at[zh, :, y], y1s.at[step], y1r.at[step], on_y(row))
        )
        y1_sends[-1].start()
    for step in range(1, 8):
        f_sends.append(remote(fl.at[y], fl.at[y], f1s.at[step], f1r.at[step], on_y(at_y(step))))
        f_sends[-1].start()
    wg[zh, :, y] = ws[4 * zh + kappa]

    def put_p1(half, j):
        piece = wg.at[half, j]
        first = remote(piece, v.at[1, half, j], p_s.at[0, half, j], p_r.at[1, half, j], ahead)
        second = remote(
            piece, v.at[2 * core, half, j], p_s.at[1, half, j], p_r.at[2 * core, half, j], jump
        )
        return first, second

    def put_p2(half, j):
        return remote(
            v.at[1, half, j], v.at[2 - 2 * core, half, j], p_s.at[2, half, j], p_r.at[2 - 2 * core, half, j], mate
        )

    def arrived(slot, half, j):
        remote(v.at[slot, half, j], v.at[slot, half, j], p_s.at[0, half, j], p_r.at[slot, half, j], ahead).wait_recv()

    for copy in y1_sends:
        copy.wait_recv()

    def start_p1(half):
        def body(j, carry):
            for copy in put_p1(half, j):
                copy.start()
            return carry

        lax.fori_loop(0, 4, body, 0)

    start_p1(zh)
    for step in range(4):
        k = lax.rem(kappa + step, 4)
        z_sends[step].wait_recv()
        for far in (4, 0):
            if step + far == 0:
                wg[oz, :, y] = zw[k]
                continue
            row = at_y(step + far)
            y2_sends.append(
                remote(zw.at[k], wg.at[oz, :, y], y2s.at[step + far], y2r.at[step + far], on_y(row))
            )
            y2_sends[-1].start()

    for copy in f_sends:
        copy.wait_recv()
    flag_sends = [
        remote(fl, fv.at[1], fxs.at[0], fxr.at[1], ahead),
        remote(fl, fv.at[2 * core], fxs.at[1], fxr.at[2 * core], jump),
    ]
    for copy in flag_sends:
        copy.start()

    def start_p2(j, carry):
        arrived(1, zh, j)
        put_p2(zh, j).start()
        return carry

    lax.fori_loop(0, 4, start_p2, 0)
    for copy in y2_sends:
        copy.wait_recv()
    start_p1(oz)

    remote(fv.at[1], fv.at[1], fxs.at[0], fxr.at[1], ahead).wait_recv()
    flag_sends.append(remote(fv.at[1], fv.at[2 - 2 * core], fxs.at[2], fxr.at[2 - 2 * core], mate))
    flag_sends[-1].start()

    first_half = lane < 64
    sign = jnp.where(first_half, 1.0, -1.0).astype(F32)

    def spread(s, carry):
        half, row = s // 8, lax.rem(s, 8)
        for j in range(4):
            value = wg[half, j, row].astype(F32)
            for h in range(2):
                one = value[:, 128 * h : 128 * h + 128]
                swapped = pltpu.roll(one, 64, 1)
                a_[s, h, 16 * j : 16 * j + 16, :] = jnp.where(first_half, one, swapped)
                b_[s, h, 16 * j : 16 * j + 16, :] = jnp.where(first_half, swapped, one)
        return carry

    lax.fori_loop(0, 16, spread, 0, unroll=2)

    def chosen(r, options):
        offset = plan[r]
        return jnp.where(offset == 1, options[0], jnp.where(offset == 2, options[1], options[2]))

    def prepare(r, j):
        def body(s, carry):
            half, row = s // 8, lax.rem(s, 8)
            value = chosen(r, [v[d, half, j, row].astype(F32) for d in range(3)])
            for h in range(2):
                one = value[:, 128 * h : 128 * h + 128]
                c_[s, h] = one * sign
                d_[s, h] = pltpu.roll(one, 64, 1)
            return carry

        lax.fori_loop(0, 16, body, 0, unroll=8)

    hops = [2 + 4 * core, 1, 7, 0]

    def cross(r, j, t, target):
        start = pl.multiple_of(8 * at_y(hops[t]), 8)
        for h in range(2):

            def body(s, totals):
                c, d = c_[s, h], d_[s, h]
                mine = [
                    a_[s, h, pl.ds(start + i, 1), :] * c + b_[s, h, pl.ds(start + i, 1), :] * d
                    for i in range(8)
                ]
                return tuple(total + one for total, one in zip(totals, mine))

            totals = lax.fori_loop(0, 16, body, (jnp.zeros((16, 128), F32),) * 8, unroll=2)
            for i in range(8):
                target[16 * i : 16 * i + 16, 128 * h : 128 * h + 128] = totals[i].astype(BF16)

    def put_cross(r, j, t):
        return remote(
            xs.at[r, j, t], xr.at[r, j, kappa], ys.at[r, j, t], yr.at[r, j, t], on_y(at_y(hops[t]))
        )

    def cross_all(r, j):
        prepare(r, j)
        for t in range(3):
            cross(r, j, t, xs.at[r, j, t])
            put_cross(r, j, t).start()
        cross(r, j, 3, xr.at[r, j, kappa])

    def put_lags(r, j):
        return remote(zs.at[r, j], zr.at[r, j], zss.at[r, j], zrr.at[r, j], other)

    def lagged(r, j, side):
        rows = pl.ds(pl.multiple_of(64 * side, 64), 64)
        total = jnp.dot(xr[r, j, 0, rows, :], lag[0], preferred_element_type=F32)
        for k in range(1, 4):
            total += jnp.dot(xr[r, j, k, rows, :], lag[k], preferred_element_type=F32)
        return total

    def lag_stage(r, j):
        for t in range(3):
            put_cross(r, j, t).wait_recv()
        zs[r, j] = lagged(r, j, oz).astype(BF16)
        put_lags(r, j).start()
        keep[r, j] = lagged(r, j, zh)

    def finish(r, j):
        put_lags(r, j).wait_recv()
        total = keep[r, j] + zr[r, j].astype(F32)
        rows = pl.ds(pl.multiple_of(16 * j, 16), 16)
        for i in range(4):
            scale = inv[r, i, rows, 0:1]
            out[r, i, rows, :] = (total[16 * i : 16 * i + 16, :] * scale)[:, :LAGS]

    def start_round(j):
        arrived(1, oz, j)
        put_p2(oz, j).start()

    start_round(0)

    wide = lax.broadcasted_iota(jnp.int32, (64, 128), 1)
    fpad[...] = jnp.zeros((128, 128), F32)
    for s in range(8):
        fpad[s : s + 1, :] = fl[s]
    fto[...] = jnp.transpose(fpad[...])
    remote(fv.at[0], fv.at[0], fxs.at[0], fxr.at[0], ahead).wait_recv()
    remote(fv.at[2], fv.at[2], fxs.at[0], fxr.at[2], ahead).wait_recv()
    table = jnp.zeros((64, 128), F32)
    for r in range(ROUNDS):
        for s in range(8):
            fpad[s : s + 1, :] = chosen(r, [fv[d, s] for d in range(3)])
        partner = jnp.transpose(fpad[...])[0:64, :]
        for i in range(8):
            number = jnp.sum(partner * fto[pl.ds(8 * y + i, 1), :], axis=1, keepdims=True)
            table = jnp.where(wide == 8 * r + i, number, table)
    ctab[...] = table
    count_send = remote(ctab, crecv, cs, cr, other)
    count_send.start()

    loads[8].wait()

    def main_loop(j, carry):
        arrived(0, zh, j)
        arrived(0, oz, j)
        arrived(2, zh, j)
        arrived(2, oz, j)
        cross_all(0, j)

        @pl.when(j < 3)
        def _():
            start_round(j + 1)

        cross_all(1, j)

        @pl.when(j == 1)
        def _():
            count_send.wait_recv()
            both = ctab[...] + crecv[...]
            for r in range(ROUNDS):
                for i in range(4):
                    number = jnp.sum(
                        jnp.where(wide == 8 * r + 4 * zh + i, both, 0.0), axis=1, keepdims=True
                    )
                    inv[r, i] = jnp.broadcast_to(1.0 / jnp.maximum(number, 1.0), (64, 128))

        @pl.when(j >= 1)
        def _():
            for r in range(ROUNDS):
                lag_stage(r, j - 1)

        @pl.when(j >= 2)
        def _():
            for r in range(ROUNDS):
                finish(r, j - 2)

        return carry

    lax.fori_loop(0, 4, main_loop, 0)
    for r in range(ROUNDS):
        lag_stage(r, 3)
    for j in (2, 3):
        for r in range(ROUNDS):
            finish(r, j)

    for copy in z_sends + y1_sends + y2_sends + f_sends + flag_sends + [count_send]:
        copy.wait_send()

    def drain(j, carry):
        for half in range(2):
            for copy in put_p1(half, j):
                copy.wait_send()
            put_p2(half, j).wait_send()
        for r in range(ROUNDS):
            for t in range(3):
                put_cross(r, j, t).wait_send()
            put_lags(r, j).wait_send()
        return carry

    lax.fori_loop(0, 4, drain, 0)


def shards(strain, validity, plan):
    t1h, t1l, t2h, t2l, twiddle = (jnp.asarray(t) for t in dft_tables())
    lag = jnp.asarray(lag_table())
    vmem = pl.BlockSpec(memory_space=pltpu.VMEM)
    dma = pltpu.SemaphoreType.DMA
    return pl.pallas_call(
        kernel,
        out_shape=jax.ShapeDtypeStruct((ROUNDS, 4, 64, LAGS), F32),
        in_specs=[pl.BlockSpec(memory_space=pltpu.HBM)] * 9,
        out_specs=vmem,
        scratch_shapes=[
            pltpu.SMEM((2,), jnp.int32),
            pltpu.VMEM((64, SAMPLES), F32),
            pltpu.VMEM((1, 64), jnp.int32),
            pltpu.VMEM((256, 256), BF16),
            pltpu.VMEM((256, 256), BF16),
            pltpu.VMEM((256, 256), BF16),
            pltpu.VMEM((256, 256), BF16),
            pltpu.VMEM((16, 128), F32),
            pltpu.VMEM((64, 1), F32),
            pltpu.VMEM((8, 64, 256), BF16),
            pltpu.VMEM((8, 64, 256), BF16),
            pltpu.VMEM((8, 64, 256), F32),
            pltpu.VMEM((8, 4, 16, 256), BF16),
            pltpu.VMEM((4, 4, 16, 256), BF16),
            pltpu.VMEM((2, 4, 8, 16, 256), BF16),
            pltpu.VMEM((3, 2, 4, 8, 16, 256), BF16),
            pltpu.VMEM((8, 1, 128), F32),
            pltpu.VMEM((3, 8, 1, 128), F32),
            pltpu.VMEM((128, 128), F32),
            pltpu.VMEM((128, 128), F32),
            pltpu.VMEM((64, 128), F32),
            pltpu.VMEM((64, 128), F32),
            pltpu.VMEM((2, 4, 64, 128), F32),
            pltpu.VMEM((16, 2, 64, 128), F32),
            pltpu.VMEM((16, 2, 64, 128), F32),
            pltpu.VMEM((16, 2, 16, 128), F32),
            pltpu.VMEM((16, 2, 16, 128), F32),
            pltpu.VMEM((2, 4, 3, 128, 256), BF16),
            pltpu.VMEM((2, 4, 4, 128, 256), BF16),
            pltpu.VMEM((4, 256, 512), BF16),
            pltpu.VMEM((2, 4, 64, 512), F32),
            pltpu.VMEM((2, 4, 64, 512), BF16),
            pltpu.VMEM((2, 4, 64, 512), BF16),
            dma((9,)),
            dma((8,)), dma((8,)),
            dma((4,)), dma((4,)),
            dma((8,)), dma((8,)),
            dma((3, 2, 4)), dma((3, 2, 4)),
            dma((8,)), dma((8,)),
            dma((3,)), dma((3,)),
            dma, dma,
            dma((2, 4, 3)), dma((2, 4, 3)),
            dma((2, 4)), dma((2, 4)),
        ],
        compiler_params=pltpu.CompilerParams(
            collective_id=0, has_side_effects=True, vmem_limit_bytes=56 * 1024 * 1024
        ),
        name="correlate",
    )(plan, strain, validity.T, t1h, t1l, t2h, t2l, twiddle, lag)


def solution(mesh):
    placed = (P("chan", "seg", None), P("chan", "seg"), P())
    return jax.shard_map(
        shards,
        mesh=mesh,
        in_specs=placed,
        out_specs=P(None, ("chan", "seg"), None, None),
        check_vma=False,
    )
```

```python
import math

import jax
import jax.numpy as jnp
import ml_dtypes
import numpy as np
from jax import lax
from jax.experimental import pallas as pl
from jax.experimental.pallas import tpu as pltpu
from jax.sharding import PartitionSpec as P

MESH = pl.DeviceIdType.MESH
SMOOTH = 32
HALF_LAGS = 200
LAGS = 2 * HALF_LAGS + 1
SAMPLES = 2048
BINS = 1024
EPSILON = 1e-05
ROUNDS = 2
F32 = jnp.float32
BF16 = jnp.bfloat16


def place(r):
    if r == 8 or r == 16:
        return 0, r // 16
    return (r, 0) if r < 8 else (16 - r, 1)


def split(table):
    high = table.astype(ml_dtypes.bfloat16)
    low = (table - high.astype(np.float64)).astype(ml_dtypes.bfloat16)
    return high, low


def dft_tables():
    c = np.arange(128)[:, None]
    q = np.arange(64)[None, :]

    def angle(steps, period):
        return 2.0 * np.pi * np.mod(steps, period) / period

    low, high = angle(c * q, 128), angle(c * (127 - q), 128)
    first = np.zeros((256, 256))
    first[:128, 0:64], first[128:, 0:64] = np.cos(low), np.sin(low)
    first[:128, 64:128], first[128:, 64:128] = -np.sin(low), np.cos(low)
    first[:128, 128:192], first[128:, 128:192] = np.cos(high), np.sin(high)
    first[:128, 192:256], first[128:, 192:256] = np.sin(high), -np.cos(high)
    eight, sixteen = angle(c * (8 + 16 * q), SAMPLES), angle(c * (16 + 16 * q), SAMPLES)
    second = np.zeros((256, 256))
    second[128:, 0:64], second[128:, 64:128] = np.cos(eight), -np.sin(eight)
    second[:128, 128:192], second[:128, 192:256] = np.cos(sixteen), -np.sin(sixteen)
    turn = angle(np.arange(8)[:, None] * np.arange(128)[None, :], SAMPLES)
    twiddle = np.concatenate([np.cos(turn), np.sin(turn)], axis=0).astype(np.float32)
    return split(first) + split(second) + (twiddle,)


def lag_table():
    lag = np.arange(-HALF_LAGS, HALF_LAGS + 1)[None, :]
    weight = 2.0 / math.sqrt(BINS)
    table = np.zeros((8, 256, 512))
    for r in range(1, 17):
        slab, half = place(r)
        turn = 2.0 * np.pi * np.mod((r + 16 * np.arange(64)[:, None]) * lag, SAMPLES) / SAMPLES
        table[slab, 128 * half : 128 * half + 64, :LAGS] = weight * np.cos(turn)
        table[slab, 128 * half + 64 : 128 * half + 128, :LAGS] = -weight * np.sin(turn)
    return table.astype(ml_dtypes.bfloat16)


def first_stage(x):
    root = math.sqrt(0.5)
    e = [x[a] + x[a + 8] for a in range(8)]
    o = [x[a] - x[a + 8] for a in range(8)]
    ee = [e[a] + e[a + 4] for a in range(4)]
    eo = [e[a] - e[a + 4] for a in range(4)]
    y = {}
    even, odd = ee[0] + ee[2], ee[1] + ee[3]
    y[0], y[8] = even + odd, even - odd
    y[4] = (ee[0] - ee[2], ee[3] - ee[1])
    minus, plus = root * (eo[1] - eo[3]), root * (eo[1] + eo[3])
    y[2] = (eo[0] + minus, -(eo[2] + plus))
    y[6] = (eo[0] - minus, eo[2] - plus)
    dm = [None] + [o[a] - o[8 - a] for a in (1, 2, 3)]
    dp = [None] + [o[a] + o[8 - a] for a in (1, 2, 3)]
    for k in (1, 3, 5, 7):
        real, imag = o[0], o[4] * math.sin(math.pi * k / 2)
        for a in (1, 2, 3):
            real = real + math.cos(2 * math.pi * a * k / 16) * dm[a]
            imag = imag + math.sin(2 * math.pi * a * k / 16) * dp[a]
        y[k] = (real, -imag)
    return y


def kernel(
    plan_in, x_in, valid_in, t1h_in, t1l_in, t2h_in, t2l_in, twiddle_in, lag_in, out,
    plan, x, flags, obuf, t1h, t1l, t2h, t2l, twiddle, valid, zh_, zl_, spec, ws, zw, wg, v, fl, fv, fpad, fto, ctab, crecv, inv,
    a_, b_, c_, d_, xs, xr, lag, keep, zs, zr,
    in_sems, out_sems, y1s, y1r, zws, zwr, y2s, y2r, p_s, p_r, f1s, f1r, fxs, fxr, cs, cr, ys, yr, zss, zrr,
):
    chan, seg = lax.axis_index("chan"), lax.axis_index("seg")
    core = lax.rem(chan, 2)
    y, zh = seg // 2, lax.rem(seg, 2)
    oz = 1 - zh
    kappa = lax.rem(y, 4)

    def at_y(step):
        return lax.rem(y + step, 8)

    def chan_at(step):
        return lax.rem(chan + step + 32, 32)

    def on_y(row):
        return (chan, 2 * row + zh)

    other = (chan, 2 * y + oz)
    ahead = (chan_at(2), seg)
    after = (chan_at(1), seg)
    mate = (chan_at(1 - 2 * core), seg)

    def remote(src, dst, send, recv, device):
        return pltpu.make_async_remote_copy(
            src_ref=src, dst_ref=dst, send_sem=send, recv_sem=recv, device_id=device, device_id_type=MESH
        )

    barrier = pltpu.get_barrier_semaphore()
    senders = [on_y(at_y(s)) for s in range(1, 8)] + [other]
    senders += [(chan_at(-1), seg), (chan_at(-2), seg), mate]
    for device in senders:
        pl.semaphore_signal(barrier, inc=1, device_id=device, device_id_type=MESH)
    strain_loads = []
    for g in range(4):
        rows = pl.ds(16 * g, 16)
        strain_loads.append(pltpu.make_async_copy(x_in.at[rows, 0, :], x.at[rows], in_sems.at[9 + g]))
        strain_loads[-1].start()
    loads = []
    pairs_in = [(twiddle_in, twiddle), (valid_in, flags), (t1h_in, t1h), (t1l_in, t1l), (t2h_in, t2h), (t2l_in, t2l)]
    pairs_in += [(plan_in, plan), (lag_in.at[pl.ds(4 * zh, 4)], lag)]
    for number, (src, dst) in enumerate(pairs_in):
        loads.append(pltpu.make_async_copy(src, dst, in_sems.at[number]))
    for copy in loads:
        copy.start()
    for copy in loads[:2]:
        copy.wait()
    square_flags = jnp.broadcast_to(flags[...].astype(F32), (64, 64))
    valid[...] = jnp.transpose(square_flags)[:, 0:1]

    def transform(g, carry):
        rows = pl.ds(pl.multiple_of(g * 16, 16), 16)
        pltpu.make_async_copy(x_in.at[rows, 0, :], x.at[rows], in_sems.at[9 + g]).wait()
        ys_ = first_stage([x[rows, 128 * s : 128 * s + 128] for s in range(16)])
        pairs = [(ys_[0], ys_[8])]
        for k in range(1, 8):
            real, imag = ys_[k]
            co, si = twiddle[k : k + 1, :], twiddle[8 + k : 9 + k, :]
            pairs.append((real * co + imag * si, imag * co - real * si))
        for j in range(8):
            for part in range(2):
                high = pairs[j][part].astype(BF16)
                zh_[j, rows, 128 * part : 128 * part + 128] = high
                zl_[j, rows, 128 * part : 128 * part + 128] = (pairs[j][part] - high.astype(F32)).astype(BF16)
        return carry

    lax.fori_loop(0, 4, transform, 0)

    for copy in loads[2:7]:
        copy.wait()

    def product(high, low, th, tl):
        total = jnp.dot(high, tl[...], preferred_element_type=F32)
        total += jnp.dot(low, th[...], preferred_element_type=F32)
        return total + jnp.dot(high, th[...], preferred_element_type=F32)

    spec[0] = product(zh_[0], zl_[0], t2h, t2l)
    main = product(zh_[1:8].reshape(448, 256), zl_[1:8].reshape(448, 256), t1h, t1l)
    spec[1:8] = main.reshape(7, 64, 256)

    lane = lax.broadcasted_iota(jnp.int32, (16, 128), 1)
    q = jnp.bitwise_and(lane, 63)

    def shifted(value, by):
        moved = pltpu.roll(value, (128 - by) % 128, 1)
        kept = q < 64 - by if by > 0 else q >= -by
        return jnp.where(kept, moved, 0.0)

    def whiten(g, carry):
        rows = pl.ds(pl.multiple_of(g * 16, 16), 16)
        mags = []
        for r in range(1, 17):
            slab, half = place(r)
            value = spec[slab, rows, 128 * half : 128 * half + 128]
            square = value * value
            mags.append(jnp.sqrt(square + pltpu.roll(square, 64, 1)))
        below, above = [mags[0]], [mags[15]]
        for r in range(1, 16):
            below.append(below[-1] + mags[r])
            above.append(above[-1] + mags[15 - r])
        above = above[::-1]
        whole = below[15]
        middle = shifted(whole, -1) + whole + shifted(whole, 1)
        weight = valid[rows, :]
        for r in range(1, 17):
            slab, half = place(r)
            window = shifted(above[r - 1], -2) + middle + shifted(below[r - 1], 2)
            factor = weight / (window * (1.0 / (2 * SMOOTH + 1)) + EPSILON)
            value = spec[slab, rows, 128 * half : 128 * half + 128]
            ws[slab, g, :, 128 * half : 128 * half + 128] = (value * factor).astype(BF16)
        return carry

    lax.fori_loop(0, 4, whiten, 0)
    column = jnp.broadcast_to(valid[...], (64, 128))
    fl[y] = jnp.transpose(jnp.concatenate([column, column], axis=0))[0:1, :]

    pl.semaphore_wait(barrier, 11)

    z_sends, y1_sends, f_sends = [], [], []
    for step in range(4):
        k = lax.rem(kappa + step, 4)
        z_sends.append(remote(ws.at[4 * oz + k], zw.at[k], zws.at[k], zwr.at[k], other))
        z_sends[-1].start()
    for step in (4, 3, 5, 2, 6, 1, 7):
        row = at_y(step)
        y1_sends.append(
            remote(ws.at[4 * zh + lax.rem(row, 4)], wg.at[zh, :, y], y1s.at[step], y1r.at[step], on_y(row))
        )
        y1_sends[-1].start()
    for step in range(1, 8):
        f_sends.append(remote(fl.at[y], fl.at[y], f1s.at[step], f1r.at[step], on_y(at_y(step))))
        f_sends[-1].start()
    wg[zh, :, y] = ws[4 * zh + kappa]

    def put_p1(half, j):
        return remote(wg.at[half, j], v.at[1, half, j], p_s.at[0, half, j], p_r.at[1, half, j], ahead)

    def put_own(half, j):
        return remote(wg.at[half, j], v.at[0, half, j], p_s.at[1, half, j], p_r.at[0, half, j], after)

    def put_on(half, j):
        return remote(v.at[1, half, j], v.at[2, half, j], p_s.at[1, half, j], p_r.at[2, half, j], after)

    def put_p2(half, j):
        return remote(
            v.at[1, half, j], v.at[2 - 2 * core, half, j], p_s.at[2, half, j], p_r.at[2 - 2 * core, half, j], mate
        )

    def start_first(half, j):
        put_p1(half, j).start()

        @pl.when(core == 0)
        def _():
            put_own(half, j).start()

    def start_second(half, j):
        arrived(1, half, j)

        @pl.when(core == 1)
        def _():
            put_on(half, j).start()

        put_p2(half, j).start()

    def arrived(slot, half, j):
        remote(v.at[slot, half, j], v.at[slot, half, j], p_s.at[0, half, j], p_r.at[slot, half, j], ahead).wait_recv()

    def put_y2(part, step):
        k = lax.rem(kappa + step, 4)
        rows = pl.ds(2 * part, 2)
        return remote(
            zw.at[k, rows], wg.at[oz, rows, y], y2s.at[part, step], y2r.at[part, step], on_y(at_y(step))
        )

    for step in range(4):
        z_sends[step].wait_recv()
        for far in (4, 0):
            if step + far > 0:
                put_y2(0, step + far).start()
    for step in (4, 5, 1, 6, 2, 7, 3):
        put_y2(1, step).start()
    wg[oz, :, y] = zw[kappa]
    for copy in y1_sends:
        copy.wait_recv()

    def start_p1(j, carry):
        start_first(zh, j)
        return carry

    lax.fori_loop(0, 4, start_p1, 0)

    for copy in f_sends:
        copy.wait_recv()
    flag_sends = [
        remote(fl, fv.at[1], fxs.at[0], fxr.at[1], ahead),
        remote(fl, fv.at[0], fxs.at[1], fxr.at[0], after),
    ]
    flag_sends[0].start()

    @pl.when(core == 0)
    def _():
        flag_sends[1].start()

    def start_direct(part):
        for step in range(1, 8):
            put_y2(part, step).wait_recv()
        for j in (2 * part, 2 * part + 1):
            start_first(oz, j)

    start_direct(0)

    def start_p2(j, carry):
        start_second(zh, j)
        return carry

    lax.fori_loop(0, 4, start_p2, 0)
    start_direct(1)
    remote(fv.at[1], fv.at[1], fxs.at[0], fxr.at[1], ahead).wait_recv()
    flag_sends.append(remote(fv.at[1], fv.at[2 - 2 * core], fxs.at[2], fxr.at[2 - 2 * core], mate))
    flag_sends[-1].start()

    @pl.when(core == 1)
    def _():
        remote(fv.at[1], fv.at[2], fxs.at[1], fxr.at[2], after).start()

    start_second(oz, 0)

    first_half = lane < 64
    sign = jnp.where(first_half, 1.0, -1.0).astype(F32)

    def spread(s, carry):
        half, row = s // 8, lax.rem(s, 8)
        for j in range(4):
            value = wg[half, j, row].astype(F32)
            for h in range(2):
                one = value[:, 128 * h : 128 * h + 128]
                swapped = pltpu.roll(one, 64, 1)
                a_[s, h, 16 * j : 16 * j + 16, :] = jnp.where(first_half, one, swapped)
                b_[s, h, 16 * j : 16 * j + 16, :] = jnp.where(first_half, swapped, one)
        return carry

    lax.fori_loop(0, 16, spread, 0, unroll=2)

    def chosen(r, options):
        offset = plan[r]
        return jnp.where(offset == 1, options[0], jnp.where(offset == 2, options[1], options[2]))

    def prepare(r, j):
        def body(s, carry):
            half, row = s // 8, lax.rem(s, 8)
            value = chosen(r, [v[d, half, j, row].astype(F32) for d in range(3)])
            for h in range(2):
                one = value[:, 128 * h : 128 * h + 128]
                c_[s, h] = one * sign
                d_[s, h] = pltpu.roll(one, 64, 1)
            return carry

        lax.fori_loop(0, 16, body, 0, unroll=8)

    hops = [2 + 4 * core, 1, 7, 0]

    def cross(r, j, t, target):
        start = pl.multiple_of(8 * at_y(hops[t]), 8)
        for h in range(2):

            def body(s, totals):
                c, d = c_[s, h], d_[s, h]
                mine = [
                    a_[s, h, pl.ds(start + i, 1), :] * c + b_[s, h, pl.ds(start + i, 1), :] * d
                    for i in range(8)
                ]
                return tuple(total + one for total, one in zip(totals, mine))

            totals = lax.fori_loop(0, 16, body, (jnp.zeros((16, 128), F32),) * 8, unroll=2)
            for i in range(8):
                target[16 * i : 16 * i + 16, 128 * h : 128 * h + 128] = totals[i].astype(BF16)

    def put_cross(r, j, t):
        return remote(
            xs.at[r, j, t], xr.at[r, j, kappa], ys.at[r, j, t], yr.at[r, j, t], on_y(at_y(hops[t]))
        )

    def cross_all(r, j):
        prepare(r, j)
        for t in range(3):
            cross(r, j, t, xs.at[r, j, t])
            put_cross(r, j, t).start()
        cross(r, j, 3, xr.at[r, j, kappa])

    def put_lags(r, j):
        return remote(zs.at[r, j], zr.at[r, j], zss.at[r, j], zrr.at[r, j], other)

    def lagged(r, j, side):
        rows = pl.ds(pl.multiple_of(64 * side, 64), 64)
        total = jnp.dot(xr[r, j, 0, rows, :], lag[0], preferred_element_type=F32)
        for k in range(1, 4):
            total += jnp.dot(xr[r, j, k, rows, :], lag[k], preferred_element_type=F32)
        return total

    def lag_stage(r, j):
        for t in range(3):
            put_cross(r, j, t).wait_recv()
        theirs = lagged(r, j, oz)
        for t in range(3):
            zs[r, j, 64 * t : 64 * t + 64, :] = theirs[:, 128 * t : 128 * t + 128].astype(BF16)
        tail = theirs[0:16, 384:512]
        for i in range(1, 4):
            tail += pltpu.roll(theirs[16 * i : 16 * i + 16, 384:512], 32 * i, 1)
        zs[r, j, 192:208, :] = tail.astype(BF16)
        put_lags(r, j).start()
        keep[r, j] = lagged(r, j, zh)

    def put_out(r, j):
        rows = pl.ds(pl.multiple_of(16 * j, 16), 16)
        return pltpu.make_async_copy(obuf.at[r, :, rows, :], out.at[r, :, rows, :], out_sems.at[r, j])

    def finish(r, j):
        put_lags(r, j).wait_recv()
        rows = pl.ds(pl.multiple_of(16 * j, 16), 16)
        tail = zr[r, j, 192:208, :].astype(F32)
        for i in range(4):
            scale = inv[r, i, rows, :]
            for t in range(3):
                theirs = zr[r, j, 64 * t + 16 * i : 64 * t + 16 * i + 16, :].astype(F32)
                mine = keep[r, j, 16 * i : 16 * i + 16, 128 * t : 128 * t + 128]
                obuf[r, i, rows, 128 * t : 128 * t + 128] = (mine + theirs) * scale
            theirs = pltpu.roll(tail, 128 - 32 * i, 1) if i else tail
            mine = keep[r, j, 16 * i : 16 * i + 16, 384:512]
            obuf[r, i, rows, 384:LAGS] = ((mine + theirs) * scale)[:, : LAGS - 384]
        put_out(r, j).start()

    start_second(oz, 1)

    wide = lax.broadcasted_iota(jnp.int32, (64, 128), 1)
    fpad[...] = jnp.zeros((128, 128), F32)
    for s in range(8):
        fpad[s : s + 1, :] = fl[s]
    fto[...] = jnp.transpose(fpad[...])
    remote(fv.at[0], fv.at[0], fxs.at[0], fxr.at[0], ahead).wait_recv()
    remote(fv.at[2], fv.at[2], fxs.at[0], fxr.at[2], ahead).wait_recv()
    table = jnp.zeros((64, 128), F32)
    for r in range(ROUNDS):
        for s in range(8):
            fpad[s : s + 1, :] = chosen(r, [fv[d, s] for d in range(3)])
        partner = jnp.transpose(fpad[...])[0:64, :]
        for i in range(8):
            number = jnp.sum(partner * fto[pl.ds(8 * y + i, 1), :], axis=1, keepdims=True)
            table = jnp.where(wide == 8 * r + i, number, table)
    ctab[...] = table
    count_send = remote(ctab, crecv, cs, cr, other)
    count_send.start()

    loads[7].wait()

    def main_loop(j, carry):
        arrived(0, zh, j)
        arrived(2, zh, j)
        arrived(0, oz, j)
        arrived(2, oz, j)
        cross_all(0, j)

        @pl.when(j < 2)
        def _():
            start_second(oz, j + 2)

        cross_all(1, j)

        @pl.when(j == 1)
        def _():
            count_send.wait_recv()
            both = ctab[...] + crecv[...]
            for r in range(ROUNDS):
                for i in range(4):
                    number = jnp.sum(
                        jnp.where(wide == 8 * r + 4 * zh + i, both, 0.0), axis=1, keepdims=True
                    )
                    inv[r, i] = jnp.broadcast_to(1.0 / jnp.maximum(number, 1.0), (64, 128))

        @pl.when(j >= 1)
        def _():
            for r in range(ROUNDS):
                lag_stage(r, j - 1)

        @pl.when(j >= 2)
        def _():
            for r in range(ROUNDS):
                finish(r, j - 2)

        return carry

    lax.fori_loop(0, 4, main_loop, 0)
    for r in range(ROUNDS):
        lag_stage(r, 3)
    for j in (2, 3):
        for r in range(ROUNDS):
            finish(r, j)

    for copy in z_sends + y1_sends + f_sends + flag_sends + [count_send]:
        copy.wait_send()

    def drain(j, carry):
        for half in range(2):
            put_p1(half, j).wait_send()
            put_own(half, j).wait_send()
            put_p2(half, j).wait_send()
        for r in range(ROUNDS):
            for t in range(3):
                put_cross(r, j, t).wait_send()
            put_lags(r, j).wait_send()
            put_out(r, j).wait()
        return carry

    lax.fori_loop(0, 4, drain, 0)
    for part in range(2):
        for step in range(1, 8):
            put_y2(part, step).wait_send()


def shards(strain, validity, plan):
    t1h, t1l, t2h, t2l, twiddle = (jnp.asarray(t) for t in dft_tables())
    lag = jnp.asarray(lag_table())
    dma = pltpu.SemaphoreType.DMA
    return pl.pallas_call(
        kernel,
        out_shape=jax.ShapeDtypeStruct((ROUNDS, 4, 64, LAGS), F32),
        in_specs=[pl.BlockSpec(memory_space=pltpu.HBM)] * 9,
        out_specs=pl.BlockSpec(memory_space=pltpu.HBM),
        scratch_shapes=[
            pltpu.SMEM((2,), jnp.int32),
            pltpu.VMEM((64, SAMPLES), F32),
            pltpu.VMEM((1, 64), jnp.int32),
            pltpu.VMEM((2, 4, 64, LAGS), F32),
            pltpu.VMEM((256, 256), BF16),
            pltpu.VMEM((256, 256), BF16),
            pltpu.VMEM((256, 256), BF16),
            pltpu.VMEM((256, 256), BF16),
            pltpu.VMEM((16, 128), F32),
            pltpu.VMEM((64, 1), F32),
            pltpu.VMEM((8, 64, 256), BF16),
            pltpu.VMEM((8, 64, 256), BF16),
            pltpu.VMEM((8, 64, 256), F32),
            pltpu.VMEM((8, 4, 16, 256), BF16),
            pltpu.VMEM((4, 4, 16, 256), BF16),
            pltpu.VMEM((2, 4, 8, 16, 256), BF16),
            pltpu.VMEM((3, 2, 4, 8, 16, 256), BF16),
            pltpu.VMEM((8, 1, 128), F32),
            pltpu.VMEM((3, 8, 1, 128), F32),
            pltpu.VMEM((128, 128), F32),
            pltpu.VMEM((128, 128), F32),
            pltpu.VMEM((64, 128), F32),
            pltpu.VMEM((64, 128), F32),
            pltpu.VMEM((2, 4, 64, 128), F32),
            pltpu.VMEM((16, 2, 64, 128), F32),
            pltpu.VMEM((16, 2, 64, 128), F32),
            pltpu.VMEM((16, 2, 16, 128), F32),
            pltpu.VMEM((16, 2, 16, 128), F32),
            pltpu.VMEM((2, 4, 3, 128, 256), BF16),
            pltpu.VMEM((2, 4, 4, 128, 256), BF16),
            pltpu.VMEM((4, 256, 512), BF16),
            pltpu.VMEM((2, 4, 64, 512), F32),
            pltpu.VMEM((2, 4, 208, 128), BF16),
            pltpu.VMEM((2, 4, 208, 128), BF16),
            dma((13,)), dma((2, 4)),
            dma((8,)), dma((8,)),
            dma((4,)), dma((4,)),
            dma((2, 8)), dma((2, 8)),
            dma((3, 2, 4)), dma((3, 2, 4)),
            dma((8,)), dma((8,)),
            dma((3,)), dma((3,)),
            dma, dma,
            dma((2, 4, 3)), dma((2, 4, 3)),
            dma((2, 4)), dma((2, 4)),
        ],
        compiler_params=pltpu.CompilerParams(
            collective_id=0, has_side_effects=True, vmem_limit_bytes=56 * 1024 * 1024
        ),
        name="correlate",
    )(plan, strain, validity.T, t1h, t1l, t2h, t2l, twiddle, lag)


def solution(mesh):
    placed = (P("chan", "seg", None), P("chan", "seg"), P())
    return jax.shard_map(
        shards,
        mesh=mesh,
        in_specs=placed,
        out_specs=P(None, ("chan", "seg"), None, None),
        check_vma=False,
    )
```

```python
import math

import jax
import jax.numpy as jnp
import ml_dtypes
import numpy as np
from jax import lax
from jax.experimental import pallas as pl
from jax.experimental.pallas import tpu as pltpu
from jax.sharding import PartitionSpec as P

MESH = pl.DeviceIdType.MESH
SMOOTH = 32
HALF_LAGS = 200
LAGS = 2 * HALF_LAGS + 1
SAMPLES = 2048
BINS = 1024
EPSILON = 1e-05
ROUNDS = 2
F32 = jnp.float32
BF16 = jnp.bfloat16


def place(r):
    if r == 8 or r == 16:
        return 0, r // 16
    return (r, 0) if r < 8 else (16 - r, 1)


def split(table):
    high = table.astype(ml_dtypes.bfloat16)
    low = (table - high.astype(np.float64)).astype(ml_dtypes.bfloat16)
    return high, low


def dft_tables():
    c = np.arange(128)[:, None]
    q = np.arange(64)[None, :]

    def angle(steps, period):
        return 2.0 * np.pi * np.mod(steps, period) / period

    low, high = angle(c * q, 128), angle(c * (127 - q), 128)
    first = np.zeros((256, 256))
    first[:128, 0:64], first[128:, 0:64] = np.cos(low), np.sin(low)
    first[:128, 64:128], first[128:, 64:128] = -np.sin(low), np.cos(low)
    first[:128, 128:192], first[128:, 128:192] = np.cos(high), np.sin(high)
    first[:128, 192:256], first[128:, 192:256] = np.sin(high), -np.cos(high)
    eight, sixteen = angle(c * (8 + 16 * q), SAMPLES), angle(c * (16 + 16 * q), SAMPLES)
    second = np.zeros((256, 256))
    second[128:, 0:64], second[128:, 64:128] = np.cos(eight), -np.sin(eight)
    second[:128, 128:192], second[:128, 192:256] = np.cos(sixteen), -np.sin(sixteen)
    turn = angle(np.arange(8)[:, None] * np.arange(128)[None, :], SAMPLES)
    twiddle = np.concatenate([np.cos(turn), np.sin(turn)], axis=0).astype(np.float32)
    return split(first) + split(second) + (twiddle,)


def lag_table():
    lag = np.arange(-HALF_LAGS, HALF_LAGS + 1)[None, :]
    weight = 2.0 / math.sqrt(BINS)
    table = np.zeros((8, 256, 512))
    for r in range(1, 17):
        slab, half = place(r)
        turn = 2.0 * np.pi * np.mod((r + 16 * np.arange(64)[:, None]) * lag, SAMPLES) / SAMPLES
        table[slab, 128 * half : 128 * half + 64, :LAGS] = weight * np.cos(turn)
        table[slab, 128 * half + 64 : 128 * half + 128, :LAGS] = -weight * np.sin(turn)
    return table.astype(ml_dtypes.bfloat16)


def first_stage(x):
    root = math.sqrt(0.5)
    e = [x[a] + x[a + 8] for a in range(8)]
    o = [x[a] - x[a + 8] for a in range(8)]
    ee = [e[a] + e[a + 4] for a in range(4)]
    eo = [e[a] - e[a + 4] for a in range(4)]
    y = {}
    even, odd = ee[0] + ee[2], ee[1] + ee[3]
    y[0], y[8] = even + odd, even - odd
    y[4] = (ee[0] - ee[2], ee[3] - ee[1])
    minus, plus = root * (eo[1] - eo[3]), root * (eo[1] + eo[3])
    y[2] = (eo[0] + minus, -(eo[2] + plus))
    y[6] = (eo[0] - minus, eo[2] - plus)
    dm = [None] + [o[a] - o[8 - a] for a in (1, 2, 3)]
    dp = [None] + [o[a] + o[8 - a] for a in (1, 2, 3)]
    for k in (1, 3, 5, 7):
        real, imag = o[0], o[4] * math.sin(math.pi * k / 2)
        for a in (1, 2, 3):
            real = real + math.cos(2 * math.pi * a * k / 16) * dm[a]
            imag = imag + math.sin(2 * math.pi * a * k / 16) * dp[a]
        y[k] = (real, -imag)
    return y


def kernel(
    plan_in, x_in, valid_in, t1h_in, t1l_in, t2h_in, t2l_in, twiddle_in, lag_in, out,
    plan, x, flags, obuf, t1h, t1l, t2h, t2l, twiddle, valid, zh_, zl_, spec, ws, zw, wg, v, fl, fv, fpad, fto, ctab, crecv, inv,
    a_, b_, c_, d_, xs, xr, lag, keep, zs, zr,
    in_sems, out_sems, y1s, y1r, zws, zwr, y2s, y2r, p_s, p_r, f1s, f1r, fxs, fxr, cs, cr, ys, yr, zss, zrr,
):
    chan, seg = lax.axis_index("chan"), lax.axis_index("seg")
    core = lax.rem(chan, 2)
    y, zh = seg // 2, lax.rem(seg, 2)
    oz = 1 - zh
    kappa = lax.rem(y, 4)

    def at_y(step):
        return lax.rem(y + step, 8)

    def chan_at(step):
        return lax.rem(chan + step + 32, 32)

    def on_y(row):
        return (chan, 2 * row + zh)

    other = (chan, 2 * y + oz)
    ahead = (chan_at(2), seg)
    after = (chan_at(1), seg)
    mate = (chan_at(1 - 2 * core), seg)

    def remote(src, dst, send, recv, device):
        return pltpu.make_async_remote_copy(
            src_ref=src, dst_ref=dst, send_sem=send, recv_sem=recv, device_id=device, device_id_type=MESH
        )

    barrier = pltpu.get_barrier_semaphore()
    senders = [on_y(at_y(s)) for s in range(1, 8)] + [other]
    senders += [(chan_at(-1), seg), (chan_at(-2), seg), mate]
    for device in senders:
        pl.semaphore_signal(barrier, inc=1, device_id=device, device_id_type=MESH)
    strain_loads = []
    for g in range(4):
        rows = pl.ds(16 * g, 16)
        strain_loads.append(pltpu.make_async_copy(x_in.at[rows, 0, :], x.at[rows], in_sems.at[9 + g]))
        strain_loads[-1].start()
    loads = []
    pairs_in = [(twiddle_in, twiddle), (valid_in, flags), (t1h_in, t1h), (t1l_in, t1l), (t2h_in, t2h), (t2l_in, t2l)]
    pairs_in += [(plan_in, plan), (lag_in.at[pl.ds(4 * zh, 4)], lag)]
    for number, (src, dst) in enumerate(pairs_in):
        loads.append(pltpu.make_async_copy(src, dst, in_sems.at[number]))
    for copy in loads:
        copy.start()
    for copy in loads[:2]:
        copy.wait()
    square_flags = jnp.broadcast_to(flags[...].astype(F32), (64, 64))
    valid[...] = jnp.transpose(square_flags)[:, 0:1]

    def transform(g, carry):
        rows = pl.ds(pl.multiple_of(g * 16, 16), 16)
        pltpu.make_async_copy(x_in.at[rows, 0, :], x.at[rows], in_sems.at[9 + g]).wait()
        ys_ = first_stage([x[rows, 128 * s : 128 * s + 128] for s in range(16)])
        pairs = [(ys_[0], ys_[8])]
        for k in range(1, 8):
            real, imag = ys_[k]
            co, si = twiddle[k : k + 1, :], twiddle[8 + k : 9 + k, :]
            pairs.append((real * co + imag * si, imag * co - real * si))
        for j in range(8):
            for part in range(2):
                high = pairs[j][part].astype(BF16)
                zh_[j, rows, 128 * part : 128 * part + 128] = high
                zl_[j, rows, 128 * part : 128 * part + 128] = (pairs[j][part] - high.astype(F32)).astype(BF16)
        return carry

    lax.fori_loop(0, 4, transform, 0)

    for copy in loads[2:7]:
        copy.wait()

    def product(high, low, th, tl):
        total = jnp.dot(high, tl[...], preferred_element_type=F32)
        total += jnp.dot(low, th[...], preferred_element_type=F32)
        return total + jnp.dot(high, th[...], preferred_element_type=F32)

    spec[0] = product(zh_[0], zl_[0], t2h, t2l)
    main = product(zh_[1:8].reshape(448, 256), zl_[1:8].reshape(448, 256), t1h, t1l)
    spec[1:8] = main.reshape(7, 64, 256)

    lane = lax.broadcasted_iota(jnp.int32, (16, 128), 1)
    q = jnp.bitwise_and(lane, 63)

    def shifted(value, by):
        moved = pltpu.roll(value, (128 - by) % 128, 1)
        kept = q < 64 - by if by > 0 else q >= -by
        return jnp.where(kept, moved, 0.0)

    def whiten(g, carry):
        rows = pl.ds(pl.multiple_of(g * 16, 16), 16)
        mags = []
        for r in range(1, 17):
            slab, half = place(r)
            value = spec[slab, rows, 128 * half : 128 * half + 128]
            square = value * value
            mags.append(jnp.sqrt(square + pltpu.roll(square, 64, 1)))
        below, above = [mags[0]], [mags[15]]
        for r in range(1, 16):
            below.append(below[-1] + mags[r])
            above.append(above[-1] + mags[15 - r])
        above = above[::-1]
        whole = below[15]
        middle = shifted(whole, -1) + whole + shifted(whole, 1)
        weight = valid[rows, :]
        for r in range(1, 17):
            slab, half = place(r)
            window = shifted(above[r - 1], -2) + middle + shifted(below[r - 1], 2)
            factor = weight / (window * (1.0 / (2 * SMOOTH + 1)) + EPSILON)
            value = spec[slab, rows, 128 * half : 128 * half + 128]
            ws[slab, g, :, 128 * half : 128 * half + 128] = (value * factor).astype(BF16)
        return carry

    lax.fori_loop(0, 4, whiten, 0)
    column = jnp.broadcast_to(valid[...], (64, 128))
    fl[y] = jnp.transpose(jnp.concatenate([column, column], axis=0))[0:1, :]

    pl.semaphore_wait(barrier, 11)

    z_sends, y1_sends, f_sends = [], [], []
    for part in range(2):
        rows = pl.ds(2 * part, 2)
        z_sends.append(
            remote(ws.at[pl.ds(4 * oz, 4), rows], zw.at[:, rows], zws.at[part], zwr.at[part], other)
        )
        z_sends[-1].start()
    for step in (4, 3, 5, 2, 6, 1, 7):
        row = at_y(step)
        y1_sends.append(
            remote(ws.at[4 * zh + lax.rem(row, 4)], wg.at[zh, :, y], y1s.at[step], y1r.at[step], on_y(row))
        )
        y1_sends[-1].start()
    for step in range(1, 8):
        f_sends.append(remote(fl.at[y], fl.at[y], f1s.at[step], f1r.at[step], on_y(at_y(step))))
        f_sends[-1].start()
    wg[zh, :, y] = ws[4 * zh + kappa]

    def put_p1(half, j):
        return remote(wg.at[half, j], v.at[1, half, j], p_s.at[0, half, j], p_r.at[1, half, j], ahead)

    def put_own(half, j):
        return remote(wg.at[half, j], v.at[0, half, j], p_s.at[1, half, j], p_r.at[0, half, j], after)

    def put_on(half, j):
        return remote(v.at[1, half, j], v.at[2, half, j], p_s.at[1, half, j], p_r.at[2, half, j], after)

    def put_p2(half, j):
        return remote(
            v.at[1, half, j], v.at[2 - 2 * core, half, j], p_s.at[2, half, j], p_r.at[2 - 2 * core, half, j], mate
        )

    def start_first(half, j):
        put_p1(half, j).start()

        @pl.when(core == 0)
        def _():
            put_own(half, j).start()

    def start_second(half, j):
        arrived(1, half, j)

        @pl.when(core == 1)
        def _():
            put_on(half, j).start()

        put_p2(half, j).start()

    def arrived(slot, half, j):
        remote(v.at[slot, half, j], v.at[slot, half, j], p_s.at[0, half, j], p_r.at[slot, half, j], ahead).wait_recv()

    def put_y2(part, step):
        k = lax.rem(kappa + step, 4)
        rows = pl.ds(2 * part, 2)
        return remote(
            zw.at[k, rows], wg.at[oz, rows, y], y2s.at[part, step], y2r.at[part, step], on_y(at_y(step))
        )

    for part in range(2):
        z_sends[part].wait_recv()
        for step in (4, 3, 5, 2, 6, 1, 7):
            put_y2(part, step).start()
    wg[oz, :, y] = zw[kappa]
    for copy in y1_sends:
        copy.wait_recv()

    start_first(zh, 0)
    start_first(zh, 1)

    for copy in f_sends:
        copy.wait_recv()
    flag_sends = [
        remote(fl, fv.at[1], fxs.at[0], fxr.at[1], ahead),
        remote(fl, fv.at[0], fxs.at[1], fxr.at[0], after),
    ]
    flag_sends[0].start()

    @pl.when(core == 0)
    def _():
        flag_sends[1].start()

    def start_direct(part):
        for step in range(1, 8):
            put_y2(part, step).wait_recv()
        for j in (2 * part, 2 * part + 1):
            start_first(oz, j)
            if part == 0:
                start_first(zh, j + 2)

    start_second(zh, 0)
    start_second(zh, 1)
    start_direct(0)
    start_direct(1)
    remote(fv.at[1], fv.at[1], fxs.at[0], fxr.at[1], ahead).wait_recv()
    flag_sends.append(remote(fv.at[1], fv.at[2 - 2 * core], fxs.at[2], fxr.at[2 - 2 * core], mate))
    flag_sends[-1].start()

    @pl.when(core == 1)
    def _():
        remote(fv.at[1], fv.at[2], fxs.at[1], fxr.at[2], after).start()

    start_second(oz, 0)

    first_half = lane < 64
    sign = jnp.where(first_half, 1.0, -1.0).astype(F32)

    def spread(s, carry):
        half, row = s // 8, lax.rem(s, 8)
        for j in range(4):
            value = wg[half, j, row].astype(F32)
            for h in range(2):
                one = value[:, 128 * h : 128 * h + 128]
                swapped = pltpu.roll(one, 64, 1)
                a_[s, h, 16 * j : 16 * j + 16, :] = jnp.where(first_half, one, swapped)
                b_[s, h, 16 * j : 16 * j + 16, :] = jnp.where(first_half, swapped, one)
        return carry

    lax.fori_loop(0, 16, spread, 0, unroll=2)

    def chosen(r, options):
        offset = plan[r]
        return jnp.where(offset == 1, options[0], jnp.where(offset == 2, options[1], options[2]))

    def prepare(r, j):
        def body(s, carry):
            half, row = s // 8, lax.rem(s, 8)
            value = chosen(r, [v[d, half, j, row].astype(F32) for d in range(3)])
            for h in range(2):
                one = value[:, 128 * h : 128 * h + 128]
                c_[s, h] = one * sign
                d_[s, h] = pltpu.roll(one, 64, 1)
            return carry

        lax.fori_loop(0, 16, body, 0, unroll=8)

    hops = [2 + 4 * core, 1, 7, 0]

    def cross(r, j, t, target):
        start = pl.multiple_of(8 * at_y(hops[t]), 8)
        for h in range(2):

            def body(s, totals):
                c, d = c_[s, h], d_[s, h]
                mine = [
                    a_[s, h, pl.ds(start + i, 1), :] * c + b_[s, h, pl.ds(start + i, 1), :] * d
                    for i in range(8)
                ]
                return tuple(total + one for total, one in zip(totals, mine))

            totals = lax.fori_loop(0, 16, body, (jnp.zeros((16, 128), F32),) * 8, unroll=2)
            for i in range(8):
                target[16 * i : 16 * i + 16, 128 * h : 128 * h + 128] = totals[i].astype(BF16)

    def put_cross(r, j, t):
        return remote(
            xs.at[r, j, t], xr.at[r, j, kappa], ys.at[r, j, t], yr.at[r, j, t], on_y(at_y(hops[t]))
        )

    def cross_all(r, j):
        prepare(r, j)
        for t in range(3):
            cross(r, j, t, xs.at[r, j, t])
            put_cross(r, j, t).start()
        cross(r, j, 3, xr.at[r, j, kappa])

    def put_lags(r, j):
        return remote(zs.at[r, j], zr.at[r, j], zss.at[r, j], zrr.at[r, j], other)

    def lagged(r, j, side):
        rows = pl.ds(pl.multiple_of(64 * side, 64), 64)
        total = jnp.dot(xr[r, j, 0, rows, :], lag[0], preferred_element_type=F32)
        for k in range(1, 4):
            total += jnp.dot(xr[r, j, k, rows, :], lag[k], preferred_element_type=F32)
        return total

    def lag_stage(r, j):
        for t in range(3):
            put_cross(r, j, t).wait_recv()
        theirs = lagged(r, j, oz)
        for t in range(3):
            zs[r, j, 64 * t : 64 * t + 64, :] = theirs[:, 128 * t : 128 * t + 128].astype(BF16)
        tail = theirs[0:16, 384:512]
        for i in range(1, 4):
            tail += pltpu.roll(theirs[16 * i : 16 * i + 16, 384:512], 32 * i, 1)
        zs[r, j, 192:208, :] = tail.astype(BF16)
        put_lags(r, j).start()

    def keep_stage(r, j):
        keep[r, j] = lagged(r, j, zh)

    def put_out(r, j):
        rows = pl.ds(pl.multiple_of(16 * j, 16), 16)
        return pltpu.make_async_copy(obuf.at[r, :, rows, :], out.at[r, :, rows, :], out_sems.at[r, j])

    def finish(r, j):
        put_lags(r, j).wait_recv()
        rows = pl.ds(pl.multiple_of(16 * j, 16), 16)
        tail = zr[r, j, 192:208, :].astype(F32)
        for i in range(4):
            scale = inv[r, i, rows, :]
            for t in range(3):
                theirs = zr[r, j, 64 * t + 16 * i : 64 * t + 16 * i + 16, :].astype(F32)
                mine = keep[r, j, 16 * i : 16 * i + 16, 128 * t : 128 * t + 128]
                obuf[r, i, rows, 128 * t : 128 * t + 128] = (mine + theirs) * scale
            theirs = pltpu.roll(tail, 128 - 32 * i, 1) if i else tail
            mine = keep[r, j, 16 * i : 16 * i + 16, 384:512]
            obuf[r, i, rows, 384:LAGS] = ((mine + theirs) * scale)[:, : LAGS - 384]
        put_out(r, j).start()

    start_second(oz, 1)

    wide = lax.broadcasted_iota(jnp.int32, (64, 128), 1)
    count_send = remote(ctab, crecv, cs, cr, other)

    def counting():
        fpad[...] = jnp.zeros((128, 128), F32)
        for s in range(8):
            fpad[s : s + 1, :] = fl[s]
        fto[...] = jnp.transpose(fpad[...])
        remote(fv.at[0], fv.at[0], fxs.at[0], fxr.at[0], ahead).wait_recv()
        remote(fv.at[2], fv.at[2], fxs.at[0], fxr.at[2], ahead).wait_recv()
        table = jnp.zeros((64, 128), F32)
        for r in range(ROUNDS):
            for s in range(8):
                fpad[s : s + 1, :] = chosen(r, [fv[d, s] for d in range(3)])
            partner = jnp.transpose(fpad[...])[0:64, :]
            for i in range(8):
                number = jnp.sum(partner * fto[pl.ds(8 * y + i, 1), :], axis=1, keepdims=True)
                table = jnp.where(wide == 8 * r + i, number, table)
        ctab[...] = table
        count_send.start()

    loads[7].wait()

    def main_loop(j, carry):
        arrived(0, zh, j)
        arrived(2, zh, j)
        arrived(0, oz, j)
        arrived(2, oz, j)

        @pl.when(j < 2)
        def _():
            start_second(zh, j + 2)

        cross_all(0, j)

        @pl.when(j < 2)
        def _():
            start_second(oz, j + 2)

        cross_all(1, j)

        @pl.when(j == 0)
        def _():
            counting()

        @pl.when(j == 2)
        def _():
            count_send.wait_recv()
            both = ctab[...] + crecv[...]
            for r in range(ROUNDS):
                for i in range(4):
                    number = jnp.sum(
                        jnp.where(wide == 8 * r + 4 * zh + i, both, 0.0), axis=1, keepdims=True
                    )
                    inv[r, i] = jnp.broadcast_to(1.0 / jnp.maximum(number, 1.0), (64, 128))

        @pl.when(j >= 1)
        def _():
            for r in range(ROUNDS):
                lag_stage(r, j - 1)
            for r in range(ROUNDS):
                keep_stage(r, j - 1)

        @pl.when(j >= 2)
        def _():
            for r in range(ROUNDS):
                finish(r, j - 2)

        return carry

    lax.fori_loop(0, 4, main_loop, 0)
    for r in range(ROUNDS):
        lag_stage(r, 3)
    for r in range(ROUNDS):
        finish(r, 2)
    for r in range(ROUNDS):
        keep_stage(r, 3)
    for r in range(ROUNDS):
        finish(r, 3)

    for copy in z_sends + y1_sends + f_sends + flag_sends + [count_send]:
        copy.wait_send()

    def drain(j, carry):
        for half in range(2):
            put_p1(half, j).wait_send()
            put_own(half, j).wait_send()
            put_p2(half, j).wait_send()
        for r in range(ROUNDS):
            for t in range(3):
                put_cross(r, j, t).wait_send()
            put_lags(r, j).wait_send()
            put_out(r, j).wait()
        return carry

    lax.fori_loop(0, 4, drain, 0)
    for part in range(2):
        for step in range(1, 8):
            put_y2(part, step).wait_send()


def shards(strain, validity, plan):
    t1h, t1l, t2h, t2l, twiddle = (jnp.asarray(t) for t in dft_tables())
    lag = jnp.asarray(lag_table())
    dma = pltpu.SemaphoreType.DMA
    return pl.pallas_call(
        kernel,
        out_shape=jax.ShapeDtypeStruct((ROUNDS, 4, 64, LAGS), F32),
        in_specs=[pl.BlockSpec(memory_space=pltpu.HBM)] * 9,
        out_specs=pl.BlockSpec(memory_space=pltpu.HBM),
        scratch_shapes=[
            pltpu.SMEM((2,), jnp.int32),
            pltpu.VMEM((64, SAMPLES), F32),
            pltpu.VMEM((1, 64), jnp.int32),
            pltpu.VMEM((2, 4, 64, LAGS), F32),
            pltpu.VMEM((256, 256), BF16),
            pltpu.VMEM((256, 256), BF16),
            pltpu.VMEM((256, 256), BF16),
            pltpu.VMEM((256, 256), BF16),
            pltpu.VMEM((16, 128), F32),
            pltpu.VMEM((64, 1), F32),
            pltpu.VMEM((8, 64, 256), BF16),
            pltpu.VMEM((8, 64, 256), BF16),
            pltpu.VMEM((8, 64, 256), F32),
            pltpu.VMEM((8, 4, 16, 256), BF16),
            pltpu.VMEM((4, 4, 16, 256), BF16),
            pltpu.VMEM((2, 4, 8, 16, 256), BF16),
            pltpu.VMEM((3, 2, 4, 8, 16, 256), BF16),
            pltpu.VMEM((8, 1, 128), F32),
            pltpu.VMEM((3, 8, 1, 128), F32),
            pltpu.VMEM((128, 128), F32),
            pltpu.VMEM((128, 128), F32),
            pltpu.VMEM((64, 128), F32),
            pltpu.VMEM((64, 128), F32),
            pltpu.VMEM((2, 4, 64, 128), F32),
            pltpu.VMEM((16, 2, 64, 128), F32),
            pltpu.VMEM((16, 2, 64, 128), F32),
            pltpu.VMEM((16, 2, 16, 128), F32),
            pltpu.VMEM((16, 2, 16, 128), F32),
            pltpu.VMEM((2, 4, 3, 128, 256), BF16),
            pltpu.VMEM((2, 4, 4, 128, 256), BF16),
            pltpu.VMEM((4, 256, 512), BF16),
            pltpu.VMEM((2, 4, 64, 512), F32),
            pltpu.VMEM((2, 4, 208, 128), BF16),
            pltpu.VMEM((2, 4, 208, 128), BF16),
            dma((13,)), dma((2, 4)),
            dma((8,)), dma((8,)),
            dma((2,)), dma((2,)),
            dma((2, 8)), dma((2, 8)),
            dma((3, 2, 4)), dma((3, 2, 4)),
            dma((8,)), dma((8,)),
            dma((3,)), dma((3,)),
            dma, dma,
            dma((2, 4, 3)), dma((2, 4, 3)),
            dma((2, 4)), dma((2, 4)),
        ],
        compiler_params=pltpu.CompilerParams(
            collective_id=0, has_side_effects=True, vmem_limit_bytes=56 * 1024 * 1024
        ),
        name="correlate",
    )(plan, strain, validity.T, t1h, t1l, t2h, t2l, twiddle, lag)


def solution(mesh):
    placed = (P("chan", "seg", None), P("chan", "seg"), P())
    return jax.shard_map(
        shards,
        mesh=mesh,
        in_specs=placed,
        out_specs=P(None, ("chan", "seg"), None, None),
        check_vma=False,
    )
```

```python
import math

import jax
import jax.numpy as jnp
import ml_dtypes
import numpy as np
from jax import lax
from jax.experimental import pallas as pl
from jax.experimental.pallas import tpu as pltpu
from jax.sharding import PartitionSpec as P

MESH = pl.DeviceIdType.MESH
SMOOTH = 32
HALF_LAGS = 200
LAGS = 2 * HALF_LAGS + 1
SAMPLES = 2048
BINS = 1024
EPSILON = 1e-05
ROUNDS = 2
F32 = jnp.float32
BF16 = jnp.bfloat16


def place(r):
    if r == 8 or r == 16:
        return 0, r // 16
    return (r, 0) if r < 8 else (16 - r, 1)


def split(table):
    high = table.astype(ml_dtypes.bfloat16)
    low = (table - high.astype(np.float64)).astype(ml_dtypes.bfloat16)
    return high, low


def dft_tables():
    c = np.arange(128)[:, None]
    q = np.arange(64)[None, :]

    def angle(steps, period):
        return 2.0 * np.pi * np.mod(steps, period) / period

    low, high = angle(c * q, 128), angle(c * (127 - q), 128)
    first = np.zeros((256, 256))
    first[:128, 0:64], first[128:, 0:64] = np.cos(low), np.sin(low)
    first[:128, 64:128], first[128:, 64:128] = -np.sin(low), np.cos(low)
    first[:128, 128:192], first[128:, 128:192] = np.cos(high), np.sin(high)
    first[:128, 192:256], first[128:, 192:256] = np.sin(high), -np.cos(high)
    eight, sixteen = angle(c * (8 + 16 * q), SAMPLES), angle(c * (16 + 16 * q), SAMPLES)
    second = np.zeros((256, 256))
    second[128:, 0:64], second[128:, 64:128] = np.cos(eight), -np.sin(eight)
    second[:128, 128:192], second[:128, 192:256] = np.cos(sixteen), -np.sin(sixteen)
    turn = angle(np.arange(8)[:, None] * np.arange(128)[None, :], SAMPLES)
    twiddle = np.concatenate([np.cos(turn), np.sin(turn)], axis=0).astype(np.float32)
    return split(first) + split(second) + (twiddle,)


def lag_table():
    lag = np.arange(-HALF_LAGS, HALF_LAGS + 1)[None, :]
    weight = 2.0 / math.sqrt(BINS)
    table = np.zeros((8, 256, 512))
    for r in range(1, 17):
        slab, half = place(r)
        turn = 2.0 * np.pi * np.mod((r + 16 * np.arange(64)[:, None]) * lag, SAMPLES) / SAMPLES
        table[slab, 128 * half : 128 * half + 64, :LAGS] = weight * np.cos(turn)
        table[slab, 128 * half + 64 : 128 * half + 128, :LAGS] = -weight * np.sin(turn)
    return table.astype(ml_dtypes.bfloat16)


def first_stage(x):
    root = math.sqrt(0.5)
    e = [x[a] + x[a + 8] for a in range(8)]
    o = [x[a] - x[a + 8] for a in range(8)]
    ee = [e[a] + e[a + 4] for a in range(4)]
    eo = [e[a] - e[a + 4] for a in range(4)]
    y = {}
    even, odd = ee[0] + ee[2], ee[1] + ee[3]
    y[0], y[8] = even + odd, even - odd
    y[4] = (ee[0] - ee[2], ee[3] - ee[1])
    minus, plus = root * (eo[1] - eo[3]), root * (eo[1] + eo[3])
    y[2] = (eo[0] + minus, -(eo[2] + plus))
    y[6] = (eo[0] - minus, eo[2] - plus)
    dm = [None] + [o[a] - o[8 - a] for a in (1, 2, 3)]
    dp = [None] + [o[a] + o[8 - a] for a in (1, 2, 3)]
    for k in (1, 3, 5, 7):
        real, imag = o[0], o[4] * math.sin(math.pi * k / 2)
        for a in (1, 2, 3):
            real = real + math.cos(2 * math.pi * a * k / 16) * dm[a]
            imag = imag + math.sin(2 * math.pi * a * k / 16) * dp[a]
        y[k] = (real, -imag)
    return y


def kernel(
    plan_in, x_in, valid_in, t1h_in, t1l_in, t2h_in, t2l_in, twiddle_in, lag_in, out,
    plan, x, flags, obuf, t1h, t1l, t2h, t2l, twiddle, valid, zh_, zl_, spec, ws, zw, wg, v, fl, fv, fpad, fto, ctab, crecv, inv,
    a_, b_, c_, d_, xs, xr, lag, keep, zs, zr,
    in_sems, out_sems, y1s, y1r, zws, zwr, y2s, y2r, p_s, p_r, f1s, f1r, fxs, fxr, cs, cr, ys, yr, zss, zrr,
):
    chan, seg = lax.axis_index("chan"), lax.axis_index("seg")
    core = lax.rem(chan, 2)
    y, zh = seg // 2, lax.rem(seg, 2)
    oz = 1 - zh
    kappa = lax.rem(y, 4)

    def at_y(step):
        return lax.rem(y + step, 8)

    def chan_at(step):
        return lax.rem(chan + step + 32, 32)

    def on_y(row):
        return (chan, 2 * row + zh)

    other = (chan, 2 * y + oz)
    ahead = (chan_at(2), seg)
    after = (chan_at(1), seg)
    mate = (chan_at(1 - 2 * core), seg)

    def remote(src, dst, send, recv, device):
        return pltpu.make_async_remote_copy(
            src_ref=src, dst_ref=dst, send_sem=send, recv_sem=recv, device_id=device, device_id_type=MESH
        )

    barrier = pltpu.get_barrier_semaphore()
    senders = [on_y(at_y(s)) for s in range(1, 8)] + [other]
    senders += [(chan_at(-1), seg), (chan_at(-2), seg), mate]
    for device in senders:
        pl.semaphore_signal(barrier, inc=1, device_id=device, device_id_type=MESH)
    strain_loads = []
    for g in range(4):
        rows = pl.ds(16 * g, 16)
        strain_loads.append(pltpu.make_async_copy(x_in.at[rows, 0, :], x.at[rows], in_sems.at[9 + g]))
        strain_loads[-1].start()
    loads = []
    pairs_in = [(twiddle_in, twiddle), (valid_in, flags), (t1h_in, t1h), (t1l_in, t1l), (t2h_in, t2h), (t2l_in, t2l)]
    pairs_in += [(plan_in, plan), (lag_in.at[pl.ds(4 * zh, 4)], lag)]
    for number, (src, dst) in enumerate(pairs_in):
        loads.append(pltpu.make_async_copy(src, dst, in_sems.at[number]))
    for copy in loads:
        copy.start()
    for copy in loads[:2]:
        copy.wait()
    square_flags = jnp.broadcast_to(flags[...].astype(F32), (64, 64))
    valid[...] = jnp.transpose(square_flags)[:, 0:1]

    def transform(g, carry):
        rows = pl.ds(pl.multiple_of(g * 16, 16), 16)
        pltpu.make_async_copy(x_in.at[rows, 0, :], x.at[rows], in_sems.at[9 + g]).wait()
        ys_ = first_stage([x[rows, 128 * s : 128 * s + 128] for s in range(16)])
        pairs = [(ys_[0], ys_[8])]
        for k in range(1, 8):
            real, imag = ys_[k]
            co, si = twiddle[k : k + 1, :], twiddle[8 + k : 9 + k, :]
            pairs.append((real * co + imag * si, imag * co - real * si))
        for j in range(8):
            for part in range(2):
                high = pairs[j][part].astype(BF16)
                zh_[j, rows, 128 * part : 128 * part + 128] = high
                zl_[j, rows, 128 * part : 128 * part + 128] = (pairs[j][part] - high.astype(F32)).astype(BF16)
        return carry

    lax.fori_loop(0, 4, transform, 0)

    for copy in loads[2:7]:
        copy.wait()

    def product(high, low, th, tl):
        total = jnp.dot(high, tl[...], preferred_element_type=F32)
        total += jnp.dot(low, th[...], preferred_element_type=F32)
        return total + jnp.dot(high, th[...], preferred_element_type=F32)

    spec[0] = product(zh_[0], zl_[0], t2h, t2l)
    main = product(zh_[1:8].reshape(448, 256), zl_[1:8].reshape(448, 256), t1h, t1l)
    spec[1:8] = main.reshape(7, 64, 256)

    lane = lax.broadcasted_iota(jnp.int32, (16, 128), 1)
    q = jnp.bitwise_and(lane, 63)

    def shifted(value, by):
        moved = pltpu.roll(value, (128 - by) % 128, 1)
        kept = q < 64 - by if by > 0 else q >= -by
        return jnp.where(kept, moved, 0.0)

    def whiten(g, carry):
        rows = pl.ds(pl.multiple_of(g * 16, 16), 16)
        mags = []
        for r in range(1, 17):
            slab, half = place(r)
            value = spec[slab, rows, 128 * half : 128 * half + 128]
            square = value * value
            mags.append(jnp.sqrt(square + pltpu.roll(square, 64, 1)))
        below, above = [mags[0]], [mags[15]]
        for r in range(1, 16):
            below.append(below[-1] + mags[r])
            above.append(above[-1] + mags[15 - r])
        above = above[::-1]
        whole = below[15]
        middle = shifted(whole, -1) + whole + shifted(whole, 1)
        weight = valid[rows, :]
        for r in range(1, 17):
            slab, half = place(r)
            window = shifted(above[r - 1], -2) + middle + shifted(below[r - 1], 2)
            factor = weight / (window * (1.0 / (2 * SMOOTH + 1)) + EPSILON)
            value = spec[slab, rows, 128 * half : 128 * half + 128]
            ws[slab, g, :, 128 * half : 128 * half + 128] = (value * factor).astype(BF16)
        return carry

    lax.fori_loop(0, 4, whiten, 0)
    column = jnp.broadcast_to(valid[...], (64, 128))
    fl[y] = jnp.transpose(jnp.concatenate([column, column], axis=0))[0:1, :]

    pl.semaphore_wait(barrier, 11)

    z_sends, y1_sends, f_sends = [], [], []
    for part in range(2):
        rows = pl.ds(2 * part, 2)
        z_sends.append(
            remote(ws.at[pl.ds(4 * oz, 4), rows], zw.at[:, rows], zws.at[part], zwr.at[part], other)
        )
        z_sends[-1].start()
    for step in (4, 3, 5, 2, 6, 1, 7):
        row = at_y(step)
        y1_sends.append(
            remote(ws.at[4 * zh + lax.rem(row, 4)], wg.at[zh, :, y], y1s.at[step], y1r.at[step], on_y(row))
        )
        y1_sends[-1].start()
    for step in range(1, 8):
        f_sends.append(remote(fl.at[y], fl.at[y], f1s.at[step], f1r.at[step], on_y(at_y(step))))
        f_sends[-1].start()
    wg[zh, :, y] = ws[4 * zh + kappa]

    def put_p1(half, j):
        return remote(wg.at[half, j], v.at[1, half, j], p_s.at[0, half, j], p_r.at[1, half, j], ahead)

    def put_own(half, j):
        return remote(wg.at[half, j], v.at[0, half, j], p_s.at[1, half, j], p_r.at[0, half, j], after)

    def put_on(half, j):
        return remote(v.at[1, half, j], v.at[2, half, j], p_s.at[1, half, j], p_r.at[2, half, j], after)

    def put_p2(half, j):
        return remote(
            v.at[1, half, j], v.at[2 - 2 * core, half, j], p_s.at[2, half, j], p_r.at[2 - 2 * core, half, j], mate
        )

    def start_first(half, j):
        put_p1(half, j).start()

        @pl.when(core == 0)
        def _():
            put_own(half, j).start()

    def start_second(half, j):
        arrived(1, half, j)

        @pl.when(core == 1)
        def _():
            put_on(half, j).start()

        put_p2(half, j).start()

    def arrived(slot, half, j):
        remote(v.at[slot, half, j], v.at[slot, half, j], p_s.at[0, half, j], p_r.at[slot, half, j], ahead).wait_recv()

    def put_y2(part, step):
        k = lax.rem(kappa + step, 4)
        rows = pl.ds(2 * part, 2)
        return remote(
            zw.at[k, rows], wg.at[oz, rows, y], y2s.at[part, step], y2r.at[part, step], on_y(at_y(step))
        )

    for part in range(2):
        z_sends[part].wait_recv()
        for step in (4, 3, 5, 2, 6, 1, 7):
            put_y2(part, step).start()
    wg[oz, :, y] = zw[kappa]
    for copy in y1_sends:
        copy.wait_recv()

    start_first(zh, 0)
    start_first(zh, 1)

    for copy in f_sends:
        copy.wait_recv()
    flag_sends = [
        remote(fl, fv.at[1], fxs.at[0], fxr.at[1], ahead),
        remote(fl, fv.at[0], fxs.at[1], fxr.at[0], after),
    ]
    flag_sends[0].start()

    @pl.when(core == 0)
    def _():
        flag_sends[1].start()

    def start_direct(part):
        for step in range(1, 8):
            put_y2(part, step).wait_recv()
        for j in (2 * part, 2 * part + 1):
            start_first(oz, j)
            if part == 0:
                start_first(zh, j + 2)

    start_second(zh, 0)
    start_second(zh, 1)
    start_direct(0)
    start_direct(1)
    remote(fv.at[1], fv.at[1], fxs.at[0], fxr.at[1], ahead).wait_recv()
    flag_sends.append(remote(fv.at[1], fv.at[2 - 2 * core], fxs.at[2], fxr.at[2 - 2 * core], mate))
    flag_sends[-1].start()

    @pl.when(core == 1)
    def _():
        remote(fv.at[1], fv.at[2], fxs.at[1], fxr.at[2], after).start()

    start_second(oz, 0)

    first_half = lane < 64
    sign = jnp.where(first_half, 1.0, -1.0).astype(F32)

    def spread(s, carry):
        half, row = s // 8, lax.rem(s, 8)
        for j in range(4):
            value = wg[half, j, row].astype(F32)
            for h in range(2):
                one = value[:, 128 * h : 128 * h + 128]
                swapped = pltpu.roll(one, 64, 1)
                a_[s, h, 16 * j : 16 * j + 16, :] = jnp.where(first_half, one, swapped)
                b_[s, h, 16 * j : 16 * j + 16, :] = jnp.where(first_half, swapped, one)
        return carry

    lax.fori_loop(0, 16, spread, 0, unroll=2)

    def chosen(r, options):
        offset = plan[r]
        return jnp.where(offset == 1, options[0], jnp.where(offset == 2, options[1], options[2]))

    def prepare(r, j):
        def body(s, carry):
            half, row = s // 8, lax.rem(s, 8)
            value = chosen(r, [v[d, half, j, row].astype(F32) for d in range(3)])
            for h in range(2):
                one = value[:, 128 * h : 128 * h + 128]
                c_[s, h] = one * sign
                d_[s, h] = pltpu.roll(one, 64, 1)
            return carry

        lax.fori_loop(0, 16, body, 0, unroll=8)

    hops = [2 + 4 * core, 1, 7, 0]

    def cross(r, j, t, target):
        start = pl.multiple_of(8 * at_y(hops[t]), 8)
        for h in range(2):

            def body(s, totals):
                c, d = c_[s, h], d_[s, h]
                mine = [
                    a_[s, h, pl.ds(start + i, 1), :] * c + b_[s, h, pl.ds(start + i, 1), :] * d
                    for i in range(8)
                ]
                return tuple(total + one for total, one in zip(totals, mine))

            totals = lax.fori_loop(0, 16, body, (jnp.zeros((16, 128), F32),) * 8, unroll=2)
            for i in range(8):
                target[16 * i : 16 * i + 16, 128 * h : 128 * h + 128] = totals[i].astype(BF16)

    def put_cross(r, j, t, part):
        rows = pl.ds(pl.multiple_of(64 * (zh if part else oz), 64), 64)
        return remote(
            xs.at[r, j, t, rows],
            xr.at[r, j, kappa, rows],
            ys.at[r, j, t, part],
            yr.at[r, j, t, part],
            on_y(at_y(hops[t])),
        )

    def cross_all(r, j):
        prepare(r, j)
        for t in range(3):
            cross(r, j, t, xs.at[r, j, t])
            put_cross(r, j, t, 0).start()
        cross(r, j, 3, xr.at[r, j, kappa])

    def put_lags(r, j):
        return remote(zs.at[r, j], zr.at[r, j], zss.at[r, j], zrr.at[r, j], other)

    def lagged(r, j, side):
        rows = pl.ds(pl.multiple_of(64 * side, 64), 64)
        total = jnp.dot(xr[r, j, 0, rows, :], lag[0], preferred_element_type=F32)
        for k in range(1, 4):
            total += jnp.dot(xr[r, j, k, rows, :], lag[k], preferred_element_type=F32)
        return total

    def lag_stage(r, j):
        for t in range(3):
            put_cross(r, j, t, 0).wait_recv()
        theirs = lagged(r, j, oz)
        for t in range(3):
            zs[r, j, 64 * t : 64 * t + 64, :] = theirs[:, 128 * t : 128 * t + 128].astype(BF16)
        tail = theirs[0:16, 384:512]
        for i in range(1, 4):
            tail += pltpu.roll(theirs[16 * i : 16 * i + 16, 384:512], 32 * i, 1)
        zs[r, j, 192:208, :] = tail.astype(BF16)
        put_lags(r, j).start()

    def keep_stage(r, j):
        for t in range(3):
            put_cross(r, j, t, 1).wait_recv()
        keep[r, j] = lagged(r, j, zh)

    def put_out(r, j):
        rows = pl.ds(pl.multiple_of(16 * j, 16), 16)
        return pltpu.make_async_copy(obuf.at[r, :, rows, :], out.at[r, :, rows, :], out_sems.at[r, j])

    def finish(r, j):
        put_lags(r, j).wait_recv()
        rows = pl.ds(pl.multiple_of(16 * j, 16), 16)
        tail = zr[r, j, 192:208, :].astype(F32)
        for i in range(4):
            scale = inv[r, i, rows, :]
            for t in range(3):
                theirs = zr[r, j, 64 * t + 16 * i : 64 * t + 16 * i + 16, :].astype(F32)
                mine = keep[r, j, 16 * i : 16 * i + 16, 128 * t : 128 * t + 128]
                obuf[r, i, rows, 128 * t : 128 * t + 128] = (mine + theirs) * scale
            theirs = pltpu.roll(tail, 128 - 32 * i, 1) if i else tail
            mine = keep[r, j, 16 * i : 16 * i + 16, 384:512]
            obuf[r, i, rows, 384:LAGS] = ((mine + theirs) * scale)[:, : LAGS - 384]
        put_out(r, j).start()

    start_second(oz, 1)

    wide = lax.broadcasted_iota(jnp.int32, (64, 128), 1)
    count_send = remote(ctab, crecv, cs, cr, other)

    def counting():
        fpad[...] = jnp.zeros((128, 128), F32)
        for s in range(8):
            fpad[s : s + 1, :] = fl[s]
        fto[...] = jnp.transpose(fpad[...])
        remote(fv.at[0], fv.at[0], fxs.at[0], fxr.at[0], ahead).wait_recv()
        remote(fv.at[2], fv.at[2], fxs.at[0], fxr.at[2], ahead).wait_recv()
        table = jnp.zeros((64, 128), F32)
        for r in range(ROUNDS):
            for s in range(8):
                fpad[s : s + 1, :] = chosen(r, [fv[d, s] for d in range(3)])
            partner = jnp.transpose(fpad[...])[0:64, :]
            for i in range(8):
                number = jnp.sum(partner * fto[pl.ds(8 * y + i, 1), :], axis=1, keepdims=True)
                table = jnp.where(wide == 8 * r + i, number, table)
        ctab[...] = table
        count_send.start()

    loads[7].wait()

    def main_loop(j, carry):
        arrived(0, zh, j)
        arrived(2, zh, j)
        arrived(0, oz, j)
        arrived(2, oz, j)

        @pl.when(j < 2)
        def _():
            start_second(zh, j + 2)

        cross_all(0, j)

        @pl.when(j < 2)
        def _():
            start_second(oz, j + 2)

        @pl.when(j >= 1)
        def _():
            lag_stage(0, j - 1)

        cross_all(1, j)
        for r in range(ROUNDS):
            for t in range(3):
                put_cross(r, j, t, 1).start()

        @pl.when(j == 0)
        def _():
            counting()

        @pl.when(j == 2)
        def _():
            count_send.wait_recv()
            both = ctab[...] + crecv[...]
            for r in range(ROUNDS):
                for i in range(4):
                    number = jnp.sum(
                        jnp.where(wide == 8 * r + 4 * zh + i, both, 0.0), axis=1, keepdims=True
                    )
                    inv[r, i] = jnp.broadcast_to(1.0 / jnp.maximum(number, 1.0), (64, 128))

        @pl.when(j >= 1)
        def _():
            lag_stage(1, j - 1)

        @pl.when(j >= 2)
        def _():
            for r in range(ROUNDS):
                keep_stage(r, j - 2)
                finish(r, j - 2)

        return carry

    lax.fori_loop(0, 4, main_loop, 0)
    for r in range(ROUNDS):
        lag_stage(r, 3)
    for r in range(ROUNDS):
        keep_stage(r, 2)
        finish(r, 2)
    for r in range(ROUNDS):
        keep_stage(r, 3)
    for r in range(ROUNDS):
        finish(r, 3)

    for copy in z_sends + y1_sends + f_sends + flag_sends + [count_send]:
        copy.wait_send()

    def drain(j, carry):
        for half in range(2):
            put_p1(half, j).wait_send()
            put_own(half, j).wait_send()
            put_p2(half, j).wait_send()
        for r in range(ROUNDS):
            for t in range(3):
                for part in range(2):
                    put_cross(r, j, t, part).wait_send()
            put_lags(r, j).wait_send()
            put_out(r, j).wait()
        return carry

    lax.fori_loop(0, 4, drain, 0)
    for part in range(2):
        for step in range(1, 8):
            put_y2(part, step).wait_send()


def shards(strain, validity, plan):
    t1h, t1l, t2h, t2l, twiddle = (jnp.asarray(t) for t in dft_tables())
    lag = jnp.asarray(lag_table())
    dma = pltpu.SemaphoreType.DMA
    return pl.pallas_call(
        kernel,
        out_shape=jax.ShapeDtypeStruct((ROUNDS, 4, 64, LAGS), F32),
        in_specs=[pl.BlockSpec(memory_space=pltpu.HBM)] * 9,
        out_specs=pl.BlockSpec(memory_space=pltpu.HBM),
        scratch_shapes=[
            pltpu.SMEM((2,), jnp.int32),
            pltpu.VMEM((64, SAMPLES), F32),
            pltpu.VMEM((1, 64), jnp.int32),
            pltpu.VMEM((2, 4, 64, LAGS), F32),
            pltpu.VMEM((256, 256), BF16),
            pltpu.VMEM((256, 256), BF16),
            pltpu.VMEM((256, 256), BF16),
            pltpu.VMEM((256, 256), BF16),
            pltpu.VMEM((16, 128), F32),
            pltpu.VMEM((64, 1), F32),
            pltpu.VMEM((8, 64, 256), BF16),
            pltpu.VMEM((8, 64, 256), BF16),
            pltpu.VMEM((8, 64, 256), F32),
            pltpu.VMEM((8, 4, 16, 256), BF16),
            pltpu.VMEM((4, 4, 16, 256), BF16),
            pltpu.VMEM((2, 4, 8, 16, 256), BF16),
            pltpu.VMEM((3, 2, 4, 8, 16, 256), BF16),
            pltpu.VMEM((8, 1, 128), F32),
            pltpu.VMEM((3, 8, 1, 128), F32),
            pltpu.VMEM((128, 128), F32),
            pltpu.VMEM((128, 128), F32),
            pltpu.VMEM((64, 128), F32),
            pltpu.VMEM((64, 128), F32),
            pltpu.VMEM((2, 4, 64, 128), F32),
            pltpu.VMEM((16, 2, 64, 128), F32),
            pltpu.VMEM((16, 2, 64, 128), F32),
            pltpu.VMEM((16, 2, 16, 128), F32),
            pltpu.VMEM((16, 2, 16, 128), F32),
            pltpu.VMEM((2, 4, 3, 128, 256), BF16),
            pltpu.VMEM((2, 4, 4, 128, 256), BF16),
            pltpu.VMEM((4, 256, 512), BF16),
            pltpu.VMEM((2, 4, 64, 512), F32),
            pltpu.VMEM((2, 4, 208, 128), BF16),
            pltpu.VMEM((2, 4, 208, 128), BF16),
            dma((13,)), dma((2, 4)),
            dma((8,)), dma((8,)),
            dma((2,)), dma((2,)),
            dma((2, 8)), dma((2, 8)),
            dma((3, 2, 4)), dma((3, 2, 4)),
            dma((8,)), dma((8,)),
            dma((3,)), dma((3,)),
            dma, dma,
            dma((2, 4, 3, 2)), dma((2, 4, 3, 2)),
            dma((2, 4)), dma((2, 4)),
        ],
        compiler_params=pltpu.CompilerParams(
            collective_id=0, has_side_effects=True, vmem_limit_bytes=56 * 1024 * 1024
        ),
        name="correlate",
    )(plan, strain, validity.T, t1h, t1l, t2h, t2l, twiddle, lag)


def solution(mesh):
    placed = (P("chan", "seg", None), P("chan", "seg"), P())
    return jax.shard_map(
        shards,
        mesh=mesh,
        in_specs=placed,
        out_specs=P(None, ("chan", "seg"), None, None),
        check_vma=False,
    )
```

```python
import math

import jax
import jax.numpy as jnp
import ml_dtypes
import numpy as np
from jax import lax
from jax.experimental import pallas as pl
from jax.experimental.pallas import tpu as pltpu
from jax.sharding import PartitionSpec as P

MESH = pl.DeviceIdType.MESH
SMOOTH = 32
HALF_LAGS = 200
LAGS = 2 * HALF_LAGS + 1
SAMPLES = 2048
BINS = 1024
EPSILON = 1e-05
ROUNDS = 2
F32 = jnp.float32
BF16 = jnp.bfloat16


def place(r):
    if r == 8 or r == 16:
        return 0, r // 16
    return (r, 0) if r < 8 else (16 - r, 1)


def split(table):
    high = table.astype(ml_dtypes.bfloat16)
    low = (table - high.astype(np.float64)).astype(ml_dtypes.bfloat16)
    return high, low


def dft_tables():
    c = np.arange(128)[:, None]
    q = np.arange(64)[None, :]

    def angle(steps, period):
        return 2.0 * np.pi * np.mod(steps, period) / period

    low, high = angle(c * q, 128), angle(c * (127 - q), 128)
    first = np.zeros((256, 256))
    first[:128, 0:64], first[128:, 0:64] = np.cos(low), np.sin(low)
    first[:128, 64:128], first[128:, 64:128] = -np.sin(low), np.cos(low)
    first[:128, 128:192], first[128:, 128:192] = np.cos(high), np.sin(high)
    first[:128, 192:256], first[128:, 192:256] = np.sin(high), -np.cos(high)
    eight, sixteen = angle(c * (8 + 16 * q), SAMPLES), angle(c * (16 + 16 * q), SAMPLES)
    second = np.zeros((256, 256))
    second[128:, 0:64], second[128:, 64:128] = np.cos(eight), -np.sin(eight)
    second[:128, 128:192], second[:128, 192:256] = np.cos(sixteen), -np.sin(sixteen)
    turn = angle(np.arange(8)[:, None] * np.arange(128)[None, :], SAMPLES)
    twiddle = np.concatenate([np.cos(turn), np.sin(turn)], axis=0).astype(np.float32)
    return split(first) + split(second) + (twiddle,)


def lag_table():
    lag = np.arange(-HALF_LAGS, HALF_LAGS + 1)[None, :]
    weight = 2.0 / math.sqrt(BINS)
    table = np.zeros((8, 256, 512))
    for r in range(1, 17):
        slab, half = place(r)
        turn = 2.0 * np.pi * np.mod((r + 16 * np.arange(64)[:, None]) * lag, SAMPLES) / SAMPLES
        table[slab, 128 * half : 128 * half + 64, :LAGS] = weight * np.cos(turn)
        table[slab, 128 * half + 64 : 128 * half + 128, :LAGS] = -weight * np.sin(turn)
    return table.astype(ml_dtypes.bfloat16)


def first_stage(x):
    root = math.sqrt(0.5)
    e = [x[a] + x[a + 8] for a in range(8)]
    o = [x[a] - x[a + 8] for a in range(8)]
    ee = [e[a] + e[a + 4] for a in range(4)]
    eo = [e[a] - e[a + 4] for a in range(4)]
    y = {}
    even, odd = ee[0] + ee[2], ee[1] + ee[3]
    y[0], y[8] = even + odd, even - odd
    y[4] = (ee[0] - ee[2], ee[3] - ee[1])
    minus, plus = root * (eo[1] - eo[3]), root * (eo[1] + eo[3])
    y[2] = (eo[0] + minus, -(eo[2] + plus))
    y[6] = (eo[0] - minus, eo[2] - plus)
    dm = [None] + [o[a] - o[8 - a] for a in (1, 2, 3)]
    dp = [None] + [o[a] + o[8 - a] for a in (1, 2, 3)]
    for k in (1, 3, 5, 7):
        real, imag = o[0], o[4] * math.sin(math.pi * k / 2)
        for a in (1, 2, 3):
            real = real + math.cos(2 * math.pi * a * k / 16) * dm[a]
            imag = imag + math.sin(2 * math.pi * a * k / 16) * dp[a]
        y[k] = (real, -imag)
    return y


def kernel(
    plan_in, x_in, valid_in, t1h_in, t1l_in, t2h_in, t2l_in, twiddle_in, lag_in, out,
    plan, x, flags, obuf, t1h, t1l, t2h, t2l, twiddle, valid, zh_, zl_, spec, ws, zw, wg, v, fl, fv, fpad, fto, ctab, crecv, inv,
    a_, b_, c_, d_, xs, xr, lag, keep, zs, zr,
    in_sems, out_sems, y1s, y1r, zws, zwr, y2s, y2r, p_s, p_r, f1s, f1r, fxs, fxr, cs, cr, ys, yr, zss, zrr,
):
    chan, seg = lax.axis_index("chan"), lax.axis_index("seg")
    core = lax.rem(chan, 2)
    y, zh = seg // 2, lax.rem(seg, 2)
    oz = 1 - zh
    kappa = lax.rem(y, 4)

    def at_y(step):
        return lax.rem(y + step, 8)

    def chan_at(step):
        return lax.rem(chan + step + 32, 32)

    def on_y(row):
        return (chan, 2 * row + zh)

    other = (chan, 2 * y + oz)
    ahead = (chan_at(2), seg)
    after = (chan_at(1), seg)
    mate = (chan_at(1 - 2 * core), seg)

    def remote(src, dst, send, recv, device):
        return pltpu.make_async_remote_copy(
            src_ref=src, dst_ref=dst, send_sem=send, recv_sem=recv, device_id=device, device_id_type=MESH
        )

    barrier = pltpu.get_barrier_semaphore()
    senders = [on_y(at_y(s)) for s in range(1, 8)] + [other]
    senders += [(chan_at(-1), seg), (chan_at(-2), seg), mate]
    for device in senders:
        pl.semaphore_signal(barrier, inc=1, device_id=device, device_id_type=MESH)
    strain_loads = []
    for g in range(4):
        rows = pl.ds(16 * g, 16)
        strain_loads.append(pltpu.make_async_copy(x_in.at[rows, 0, :], x.at[rows], in_sems.at[9 + g]))
        strain_loads[-1].start()
    loads = []
    pairs_in = [(twiddle_in, twiddle), (valid_in, flags), (t1h_in, t1h), (t1l_in, t1l), (t2h_in, t2h), (t2l_in, t2l)]
    pairs_in += [(plan_in, plan), (lag_in.at[pl.ds(4 * zh, 4)], lag)]
    for number, (src, dst) in enumerate(pairs_in):
        loads.append(pltpu.make_async_copy(src, dst, in_sems.at[number]))
    for copy in loads:
        copy.start()
    for copy in loads[:2]:
        copy.wait()
    square_flags = jnp.broadcast_to(flags[...].astype(F32), (64, 64))
    valid[...] = jnp.transpose(square_flags)[:, 0:1]

    def transform(g, carry):
        rows = pl.ds(pl.multiple_of(g * 16, 16), 16)
        pltpu.make_async_copy(x_in.at[rows, 0, :], x.at[rows], in_sems.at[9 + g]).wait()
        ys_ = first_stage([x[rows, 128 * s : 128 * s + 128] for s in range(16)])
        pairs = [(ys_[0], ys_[8])]
        for k in range(1, 8):
            real, imag = ys_[k]
            co, si = twiddle[k : k + 1, :], twiddle[8 + k : 9 + k, :]
            pairs.append((real * co + imag * si, imag * co - real * si))
        for j in range(8):
            for part in range(2):
                high = pairs[j][part].astype(BF16)
                zh_[j, rows, 128 * part : 128 * part + 128] = high
                zl_[j, rows, 128 * part : 128 * part + 128] = (pairs[j][part] - high.astype(F32)).astype(BF16)
        return carry

    lax.fori_loop(0, 4, transform, 0)

    for copy in loads[2:7]:
        copy.wait()

    def product(high, low, th, tl):
        total = jnp.dot(high, tl[...], preferred_element_type=F32)
        total += jnp.dot(low, th[...], preferred_element_type=F32)
        return total + jnp.dot(high, th[...], preferred_element_type=F32)

    spec[0] = product(zh_[0], zl_[0], t2h, t2l)
    main = product(zh_[1:8].reshape(448, 256), zl_[1:8].reshape(448, 256), t1h, t1l)
    spec[1:8] = main.reshape(7, 64, 256)

    lane = lax.broadcasted_iota(jnp.int32, (16, 128), 1)
    q = jnp.bitwise_and(lane, 63)

    def shifted(value, by):
        moved = pltpu.roll(value, (128 - by) % 128, 1)
        kept = q < 64 - by if by > 0 else q >= -by
        return jnp.where(kept, moved, 0.0)

    def whiten(g, carry):
        rows = pl.ds(pl.multiple_of(g * 16, 16), 16)
        mags = []
        for r in range(1, 17):
            slab, half = place(r)
            value = spec[slab, rows, 128 * half : 128 * half + 128]
            square = value * value
            mags.append(jnp.sqrt(square + pltpu.roll(square, 64, 1)))
        below, above = [mags[0]], [mags[15]]
        for r in range(1, 16):
            below.append(below[-1] + mags[r])
            above.append(above[-1] + mags[15 - r])
        above = above[::-1]
        whole = below[15]
        middle = shifted(whole, -1) + whole + shifted(whole, 1)
        weight = valid[rows, :]
        for r in range(1, 17):
            slab, half = place(r)
            window = shifted(above[r - 1], -2) + middle + shifted(below[r - 1], 2)
            factor = weight / (window * (1.0 / (2 * SMOOTH + 1)) + EPSILON)
            value = spec[slab, rows, 128 * half : 128 * half + 128]
            ws[slab, g, :, 128 * half : 128 * half + 128] = (value * factor).astype(BF16)
        return carry

    lax.fori_loop(0, 4, whiten, 0)
    column = jnp.broadcast_to(valid[...], (64, 128))
    fl[y] = jnp.transpose(jnp.concatenate([column, column], axis=0))[0:1, :]

    pl.semaphore_wait(barrier, 11)

    z_sends, y1_sends, f_sends = [], [], []
    for part in range(2):
        rows = pl.ds(2 * part, 2)
        z_sends.append(
            remote(ws.at[pl.ds(4 * oz, 4), rows], zw.at[:, rows], zws.at[part], zwr.at[part], other)
        )
        z_sends[-1].start()
    for step in (4, 3, 5, 2, 6, 1, 7):
        row = at_y(step)
        y1_sends.append(
            remote(ws.at[4 * zh + lax.rem(row, 4)], wg.at[zh, :, y], y1s.at[step], y1r.at[step], on_y(row))
        )
        y1_sends[-1].start()
    for step in range(1, 8):
        f_sends.append(remote(fl.at[y], fl.at[y], f1s.at[step], f1r.at[step], on_y(at_y(step))))
        f_sends[-1].start()
    wg[zh, :, y] = ws[4 * zh + kappa]

    def put_p1(half, j):
        return remote(wg.at[half, j], v.at[1, half, j], p_s.at[0, half, j], p_r.at[1, half, j], ahead)

    def put_own(half, j):
        return remote(wg.at[half, j], v.at[0, half, j], p_s.at[1, half, j], p_r.at[0, half, j], after)

    def put_on(half, j):
        return remote(v.at[1, half, j], v.at[2, half, j], p_s.at[1, half, j], p_r.at[2, half, j], after)

    def put_p2(half, j):
        return remote(
            v.at[1, half, j], v.at[2 - 2 * core, half, j], p_s.at[2, half, j], p_r.at[2 - 2 * core, half, j], mate
        )

    def start_first(half, j):
        put_p1(half, j).start()

        @pl.when(core == 0)
        def _():
            put_own(half, j).start()

    def start_second(half, j):
        arrived(1, half, j)

        @pl.when(core == 1)
        def _():
            put_on(half, j).start()

        put_p2(half, j).start()

    def arrived(slot, half, j):
        remote(v.at[slot, half, j], v.at[slot, half, j], p_s.at[0, half, j], p_r.at[slot, half, j], ahead).wait_recv()

    def put_y2(part, step):
        k = lax.rem(kappa + step, 4)
        rows = pl.ds(2 * part, 2)
        return remote(
            zw.at[k, rows], wg.at[oz, rows, y], y2s.at[part, step], y2r.at[part, step], on_y(at_y(step))
        )

    for part in range(2):
        z_sends[part].wait_recv()
        for step in (4, 3, 5, 2, 6, 1, 7):
            put_y2(part, step).start()
    wg[oz, :, y] = zw[kappa]
    for copy in y1_sends:
        copy.wait_recv()

    start_first(zh, 0)
    start_first(zh, 1)

    for copy in f_sends:
        copy.wait_recv()
    flag_sends = [
        remote(fl, fv.at[1], fxs.at[0], fxr.at[1], ahead),
        remote(fl, fv.at[0], fxs.at[1], fxr.at[0], after),
    ]
    flag_sends[0].start()

    @pl.when(core == 0)
    def _():
        flag_sends[1].start()

    def start_direct(part):
        for step in range(1, 8):
            put_y2(part, step).wait_recv()
        for j in (2 * part, 2 * part + 1):
            start_first(oz, j)
            if part == 0:
                start_first(zh, j + 2)

    start_second(zh, 0)
    start_second(zh, 1)
    start_direct(0)
    start_direct(1)
    remote(fv.at[1], fv.at[1], fxs.at[0], fxr.at[1], ahead).wait_recv()
    flag_sends.append(remote(fv.at[1], fv.at[2 - 2 * core], fxs.at[2], fxr.at[2 - 2 * core], mate))
    flag_sends[-1].start()

    @pl.when(core == 1)
    def _():
        remote(fv.at[1], fv.at[2], fxs.at[1], fxr.at[2], after).start()

    start_second(oz, 0)

    first_half = lane < 64
    sign = jnp.where(first_half, 1.0, -1.0).astype(F32)

    def spread(s, carry):
        half, row = s // 8, lax.rem(s, 8)
        for j in range(4):
            value = wg[half, j, row].astype(F32)
            for h in range(2):
                one = value[:, 128 * h : 128 * h + 128]
                swapped = pltpu.roll(one, 64, 1)
                a_[s, h, 16 * j : 16 * j + 16, :] = jnp.where(first_half, one, swapped)
                b_[s, h, 16 * j : 16 * j + 16, :] = jnp.where(first_half, swapped, one)
        return carry

    lax.fori_loop(0, 16, spread, 0, unroll=2)

    def chosen(r, options):
        offset = plan[r]
        return jnp.where(offset == 1, options[0], jnp.where(offset == 2, options[1], options[2]))

    def prepare(r, j):
        def body(s, carry):
            half, row = s // 8, lax.rem(s, 8)
            value = chosen(r, [v[d, half, j, row].astype(F32) for d in range(3)])
            for h in range(2):
                one = value[:, 128 * h : 128 * h + 128]
                c_[s, h] = one * sign
                d_[s, h] = pltpu.roll(one, 64, 1)
            return carry

        lax.fori_loop(0, 16, body, 0, unroll=8)

    hops = [2 + 4 * core, 1, 7, 0]

    def cross(r, j, t, target):
        start = pl.multiple_of(8 * at_y(hops[t]), 8)
        for h in range(2):

            def body(s, totals):
                c, d = c_[s, h], d_[s, h]
                mine = [
                    a_[s, h, pl.ds(start + i, 1), :] * c + b_[s, h, pl.ds(start + i, 1), :] * d
                    for i in range(8)
                ]
                return tuple(total + one for total, one in zip(totals, mine))

            totals = lax.fori_loop(0, 16, body, (jnp.zeros((16, 128), F32),) * 8, unroll=2)
            for i in range(8):
                target[16 * i : 16 * i + 16, 128 * h : 128 * h + 128] = totals[i].astype(BF16)

    def put_cross(r, j, t, part):
        rows = pl.ds(pl.multiple_of(64 * (zh if part else oz), 64), 64)
        return remote(
            xs.at[r, j, t, rows],
            xr.at[r, j, kappa, rows],
            ys.at[r, j, t, part],
            yr.at[r, j, t, part],
            on_y(at_y(hops[t])),
        )

    def cross_all(r, j):
        prepare(r, j)
        for t in range(3):
            cross(r, j, t, xs.at[r, j, t])
            put_cross(r, j, t, 0).start()
        cross(r, j, 3, xr.at[r, j, kappa])

    def put_lags(r, j):
        return remote(zs.at[r, j], zr.at[r, j], zss.at[r, j], zrr.at[r, j], other)

    def lagged(r, j, side):
        rows = pl.ds(pl.multiple_of(64 * side, 64), 64)
        total = jnp.dot(xr[r, j, 0, rows, :], lag[0], preferred_element_type=F32)
        for k in range(1, 4):
            total += jnp.dot(xr[r, j, k, rows, :], lag[k], preferred_element_type=F32)
        return total

    def lag_stage(r, j):
        for t in range(3):
            put_cross(r, j, t, 0).wait_recv()
        theirs = lagged(r, j, oz)
        for t in range(3):
            zs[r, j, 64 * t : 64 * t + 64, :] = theirs[:, 128 * t : 128 * t + 128].astype(BF16)
        tail = theirs[0:16, 384:512]
        for i in range(1, 4):
            tail += pltpu.roll(theirs[16 * i : 16 * i + 16, 384:512], 32 * i, 1)
        zs[r, j, 192:208, :] = tail.astype(BF16)
        put_lags(r, j).start()

    def keep_stage(r, j):
        for t in range(3):
            put_cross(r, j, t, 1).wait_recv()
        keep[r, j] = lagged(r, j, zh)

    def put_out(r, j):
        rows = pl.ds(pl.multiple_of(16 * j, 16), 16)
        return pltpu.make_async_copy(obuf.at[r, :, rows, :], out.at[r, :, rows, :], out_sems.at[r, j])

    def finish(r, j):
        put_lags(r, j).wait_recv()
        rows = pl.ds(pl.multiple_of(16 * j, 16), 16)
        tail = zr[r, j, 192:208, :].astype(F32)
        for i in range(4):
            scale = inv[r, i, rows, :]
            for t in range(3):
                theirs = zr[r, j, 64 * t + 16 * i : 64 * t + 16 * i + 16, :].astype(F32)
                mine = keep[r, j, 16 * i : 16 * i + 16, 128 * t : 128 * t + 128]
                obuf[r, i, rows, 128 * t : 128 * t + 128] = (mine + theirs) * scale
            theirs = pltpu.roll(tail, 128 - 32 * i, 1) if i else tail
            mine = keep[r, j, 16 * i : 16 * i + 16, 384:512]
            obuf[r, i, rows, 384:LAGS] = ((mine + theirs) * scale)[:, : LAGS - 384]
        put_out(r, j).start()

    start_second(oz, 1)

    wide = lax.broadcasted_iota(jnp.int32, (64, 128), 1)
    count_send = remote(ctab, crecv, cs, cr, other)

    def counting():
        fpad[...] = jnp.zeros((128, 128), F32)
        for s in range(8):
            fpad[s : s + 1, :] = fl[s]
        fto[...] = jnp.transpose(fpad[...])
        remote(fv.at[0], fv.at[0], fxs.at[0], fxr.at[0], ahead).wait_recv()
        remote(fv.at[2], fv.at[2], fxs.at[0], fxr.at[2], ahead).wait_recv()
        table = jnp.zeros((64, 128), F32)
        for r in range(ROUNDS):
            for s in range(8):
                fpad[s : s + 1, :] = chosen(r, [fv[d, s] for d in range(3)])
            partner = jnp.transpose(fpad[...])[0:64, :]
            for i in range(8):
                number = jnp.sum(partner * fto[pl.ds(8 * y + i, 1), :], axis=1, keepdims=True)
                table = jnp.where(wide == 8 * r + i, number, table)
        ctab[...] = table
        count_send.start()

    loads[7].wait()

    def main_loop(j, carry):
        arrived(0, zh, j)
        arrived(2, zh, j)
        arrived(0, oz, j)
        arrived(2, oz, j)

        @pl.when(j < 2)
        def _():
            start_second(zh, j + 2)

        cross_all(0, j)

        @pl.when(j < 2)
        def _():
            start_second(oz, j + 2)

        @pl.when(j >= 1)
        def _():
            lag_stage(0, j - 1)
            lag_stage(1, j - 1)

        cross_all(1, j)
        for r in range(ROUNDS):
            for t in range(3):
                put_cross(r, j, t, 1).start()

        @pl.when(j == 0)
        def _():
            counting()

        @pl.when(j == 2)
        def _():
            count_send.wait_recv()
            both = ctab[...] + crecv[...]
            for r in range(ROUNDS):
                for i in range(4):
                    number = jnp.sum(
                        jnp.where(wide == 8 * r + 4 * zh + i, both, 0.0), axis=1, keepdims=True
                    )
                    inv[r, i] = jnp.broadcast_to(1.0 / jnp.maximum(number, 1.0), (64, 128))

        @pl.when(j >= 2)
        def _():
            for r in range(ROUNDS):
                keep_stage(r, j - 2)
                finish(r, j - 2)

        return carry

    lax.fori_loop(0, 4, main_loop, 0)
    for r in range(ROUNDS):
        lag_stage(r, 3)
    for r in range(ROUNDS):
        keep_stage(r, 2)
        finish(r, 2)
    for r in range(ROUNDS):
        keep_stage(r, 3)
    for r in range(ROUNDS):
        finish(r, 3)

    for copy in z_sends + y1_sends + f_sends + flag_sends + [count_send]:
        copy.wait_send()

    def drain(j, carry):
        for half in range(2):
            put_p1(half, j).wait_send()
            put_own(half, j).wait_send()
            put_p2(half, j).wait_send()
        for r in range(ROUNDS):
            for t in range(3):
                for part in range(2):
                    put_cross(r, j, t, part).wait_send()
            put_lags(r, j).wait_send()
            put_out(r, j).wait()
        return carry

    lax.fori_loop(0, 4, drain, 0)
    for part in range(2):
        for step in range(1, 8):
            put_y2(part, step).wait_send()


def shards(strain, validity, plan):
    t1h, t1l, t2h, t2l, twiddle = (jnp.asarray(t) for t in dft_tables())
    lag = jnp.asarray(lag_table())
    dma = pltpu.SemaphoreType.DMA
    return pl.pallas_call(
        kernel,
        out_shape=jax.ShapeDtypeStruct((ROUNDS, 4, 64, LAGS), F32),
        in_specs=[pl.BlockSpec(memory_space=pltpu.HBM)] * 9,
        out_specs=pl.BlockSpec(memory_space=pltpu.HBM),
        scratch_shapes=[
            pltpu.SMEM((2,), jnp.int32),
            pltpu.VMEM((64, SAMPLES), F32),
            pltpu.VMEM((1, 64), jnp.int32),
            pltpu.VMEM((2, 4, 64, LAGS), F32),
            pltpu.VMEM((256, 256), BF16),
            pltpu.VMEM((256, 256), BF16),
            pltpu.VMEM((256, 256), BF16),
            pltpu.VMEM((256, 256), BF16),
            pltpu.VMEM((16, 128), F32),
            pltpu.VMEM((64, 1), F32),
            pltpu.VMEM((8, 64, 256), BF16),
            pltpu.VMEM((8, 64, 256), BF16),
            pltpu.VMEM((8, 64, 256), F32),
            pltpu.VMEM((8, 4, 16, 256), BF16),
            pltpu.VMEM((4, 4, 16, 256), BF16),
            pltpu.VMEM((2, 4, 8, 16, 256), BF16),
            pltpu.VMEM((3, 2, 4, 8, 16, 256), BF16),
            pltpu.VMEM((8, 1, 128), F32),
            pltpu.VMEM((3, 8, 1, 128), F32),
            pltpu.VMEM((128, 128), F32),
            pltpu.VMEM((128, 128), F32),
            pltpu.VMEM((64, 128), F32),
            pltpu.VMEM((64, 128), F32),
            pltpu.VMEM((2, 4, 64, 128), F32),
            pltpu.VMEM((16, 2, 64, 128), F32),
            pltpu.VMEM((16, 2, 64, 128), F32),
            pltpu.VMEM((16, 2, 16, 128), F32),
            pltpu.VMEM((16, 2, 16, 128), F32),
            pltpu.VMEM((2, 4, 3, 128, 256), BF16),
            pltpu.VMEM((2, 4, 4, 128, 256), BF16),
            pltpu.VMEM((4, 256, 512), BF16),
            pltpu.VMEM((2, 4, 64, 512), F32),
            pltpu.VMEM((2, 4, 208, 128), BF16),
            pltpu.VMEM((2, 4, 208, 128), BF16),
            dma((13,)), dma((2, 4)),
            dma((8,)), dma((8,)),
            dma((2,)), dma((2,)),
            dma((2, 8)), dma((2, 8)),
            dma((3, 2, 4)), dma((3, 2, 4)),
            dma((8,)), dma((8,)),
            dma((3,)), dma((3,)),
            dma, dma,
            dma((2, 4, 3, 2)), dma((2, 4, 3, 2)),
            dma((2, 4)), dma((2, 4)),
        ],
        compiler_params=pltpu.CompilerParams(
            collective_id=0, has_side_effects=True, vmem_limit_bytes=56 * 1024 * 1024
        ),
        name="correlate",
    )(plan, strain, validity.T, t1h, t1l, t2h, t2l, twiddle, lag)


def solution(mesh):
    placed = (P("chan", "seg", None), P("chan", "seg"), P())
    return jax.shard_map(
        shards,
        mesh=mesh,
        in_specs=placed,
        out_specs=P(None, ("chan", "seg"), None, None),
        check_vma=False,
    )
```
